256 devices in a mesh: seq: 16 (over y, x_lo, core), rep: 16 (over x_hi, z).
Axes of the slice: x: 4 (x_hi: 2, x_lo: 2; x = x_hi * 2 + x_lo), y: 4, z: 8, core: 2. Of those that a mesh axis runs over, the one named last changes fastest.
Arguments:
- queries: bfloat16 [16, 4096, 16, 128], P('rep', 'seq'), may hold values from -12 to 12
- keys: bfloat16 [16, 4096, 16, 128], P('rep', 'seq'), may hold values from -6 to 6
- values: bfloat16 [16, 4096, 16, 128], P('rep', 'seq'), may hold values from -6 to 6
- w_proj: bfloat16 [2048, 512], replicated, may hold values from -0.25 to 0.25
- norm_gain: float32 [512], replicated, may hold values from 0.5 to 1.5
- norm_bias: float32 [512], replicated, may hold values from -3 to 3
- conv_weight: bfloat16 [3, 3, 3, 512, 512], P(None, None, None, None, 'rep'), may hold values from -0.0546875 to 0.0546875
- conv_bias: float32 [512], P('rep'), may hold values from -3 to 3
Outputs:
- decoded: bfloat16 [16, 16, 4, 8, 8, 512], P(None, 'seq', None, None, None, 'rep')
The draws below stay inside these ranges and needn't reach their ends.
All inputs are finite; a program needn't handle non-finite values.
Results may differ from the reference program's by a relative error of at most 0.0059.
Values may be sent and summed in bfloat16 or wider, within the bound.
A program may use at most 128 MiB of HBM per device.

```python
import jax
import jax.numpy as jnp
from jax import lax

HEADS = 16
HD = 128
C = 512
GROUPS = 32
FRAMES = 4
TH = 8
TW = 8
VIDEOS = 16
LEN = 4096
N_SEQ = 16


def draw_queries(key, part):
    key = jax.random.fold_in(key, 11)
    position = jnp.arange(LEN)
    ramp = 1.0 + 2.0 * position.astype(jnp.float32) / max(LEN - 1, 1)
    result = jnp.clip(jax.random.normal(key, (VIDEOS, LEN, HEADS, HD), jnp.float32), -4.0, 4.0)
    result = result * ramp[None, :, None, None]
    return result.astype(jnp.bfloat16)


def draw_keys(key, part):
    key = jax.random.fold_in(key, 12)
    result = jnp.clip(jax.random.normal(key, (VIDEOS, LEN, HEADS, HD), jnp.float32), -6.0, 6.0)
    return result.astype(jnp.bfloat16)


def block_scale(key, shape, cuts, least, top_value):
    def one(dim, parts):
        steps = jax.random.uniform(jax.random.fold_in(jax.random.fold_in(key, 6), dim), (parts,), jnp.float32, least / len(cuts), top_value / len(cuts))
        return jnp.repeat(jnp.exp(steps), shape[dim] // parts).reshape((-1,) + (1,) * (len(shape) - dim - 1))

    gain = one(*cuts[0])
    for cut in cuts[1:]:
        gain = gain * one(*cut)
    return gain


def scatter_about(stream_key, dims, scale, limit, split=(), kind=jnp.bfloat16):
    loudness = block_scale(stream_key, dims, split, -0.22, 0.18) if split else 1.0
    values = jax.random.normal(stream_key, dims, jnp.float32) * scale * loudness
    return jnp.minimum(jnp.maximum(values, -limit), limit).astype(kind)


def setup_inputs(seed: int = 0) -> dict:
    splits = jax.random.split(jax.random.key(seed), 9)
    return {
        "queries": draw_queries(jax.random.fold_in(splits[8], 71), 0),
        "keys": draw_keys(jax.random.fold_in(splits[8], 71), 0),
        "values": scatter_about(splits[2], (VIDEOS, LEN, HEADS, HD), 1.0, 6.0, ((0, 16), (1, 16))),
        "w_proj": scatter_about(splits[3], (HEADS * HD, C), (HEADS * HD // 4) ** -0.5, 0.25),
        "norm_gain": jnp.clip(1.0 + 0.1 * jax.random.normal(splits[4], (C,), jnp.float32), 0.5, 1.5),
        "norm_bias": scatter_about(splits[5], (C,), 0.5, 3.0, (), jnp.float32),
        "conv_weight": scatter_about(splits[6], (3, 3, 3, C, C), (27 * C) ** -0.5, 0.0546875, ((4, 16),)),
        "conv_bias": scatter_about(splits[7], (C,), 0.5, 3.0, ((0, 16),), jnp.float32),
    }


def attend(query_video, key_video, value_video):
    block = min(512, LEN)
    scale = HD ** (-0.5)
    blocks = query_video.reshape(LEN // block, block, HEADS, HD)
    key_full = key_video.astype(jnp.float32)
    value_full = value_video.astype(jnp.float32)

    def one_block(query_block):
        scores = jnp.einsum('qhd,khd->hqk', query_block.astype(jnp.float32), key_full) * scale
        top = lax.optimization_barrier(jnp.max(scores, axis=-1, keepdims=True))
        expd = jnp.exp(scores - top)
        total = lax.optimization_barrier(jnp.sum(expd, axis=-1, keepdims=True))
        weights = lax.optimization_barrier((expd / total).astype(jnp.bfloat16))
        mixed = jnp.einsum('hqk,khd->qhd', weights.astype(jnp.float32), value_full)
        return mixed.astype(jnp.bfloat16)
    return lax.map(one_block, blocks).reshape(LEN, HEADS, HD)

def to_grid(tiles, tile_rows, tile_cols):
    shaped = tiles.reshape(tile_rows, tile_cols, FRAMES, TH, TW, C)
    return shaped.transpose(2, 0, 3, 1, 4, 5).reshape(FRAMES, tile_rows * TH, tile_cols * TW, C)

def to_tiles(field, tile_rows, tile_cols):
    shaped = field.reshape(FRAMES, tile_rows, TH, tile_cols, TW, C)
    return shaped.transpose(1, 3, 0, 2, 4, 5).reshape(N_SEQ, FRAMES, TH, TW, C)

def decode_video(latent, norm_gain, norm_bias, conv_weight, conv_bias):
    tile_cols = min(4, N_SEQ // 2)
    tile_rows = N_SEQ // tile_cols
    height = tile_rows * TH
    width = tile_cols * TW
    group_size = C // GROUPS
    grid = to_grid(latent.reshape(N_SEQ, FRAMES, TH, TW, C), tile_rows, tile_cols)
    wide = lax.optimization_barrier(grid).astype(jnp.float32)
    grouped = wide.reshape(FRAMES, height, width, GROUPS, group_size)
    count = FRAMES * height * width * group_size
    mean = lax.optimization_barrier(jnp.sum(grouped, axis=(0, 1, 2, 4))) / count
    square = lax.optimization_barrier(jnp.sum(grouped * grouped, axis=(0, 1, 2, 4))) / count
    var = square - mean * mean
    inverse = lax.rsqrt(var + 1e-06)
    normed = (grouped - mean[:, None]) * inverse[:, None]
    normed = normed.reshape(FRAMES, height, width, C) * norm_gain + norm_bias
    activated = lax.optimization_barrier(jax.nn.silu(normed).astype(jnp.bfloat16))
    padded = jnp.pad(activated.astype(jnp.float32), ((2, 0), (1, 1), (1, 1), (0, 0)))
    kernel = conv_weight.astype(jnp.float32)
    accum = jnp.zeros((FRAMES, height, width, C), jnp.float32)
    for depth in range(3):
        for row_tap in range(3):
            for col_tap in range(3):
                window = padded[depth:depth + FRAMES, row_tap:row_tap + height, col_tap:col_tap + width, :]
                accum = accum + jnp.einsum('fhwc,co->fhwo', window, kernel[depth, row_tap, col_tap])
    result = (wide + accum + conv_bias).astype(jnp.bfloat16)
    return to_tiles(result, tile_rows, tile_cols)

def reference(queries, keys, values, w_proj, norm_gain, norm_bias, conv_weight, conv_bias):

    def one_video(triple):
        attended = attend(triple[0], triple[1], triple[2])
        flat = attended.reshape(LEN, HEADS * HD)
        latent = jnp.dot(flat, w_proj, preferred_element_type=jnp.float32).astype(jnp.bfloat16)
        return decode_video(latent, norm_gain, norm_bias, conv_weight, conv_bias)
    return lax.map(one_video, (queries, keys, values))
```

```python
import math

import jax
import jax.numpy as jnp
from jax import lax
from jax.experimental import pallas as pl
from jax.experimental.pallas import tpu as pltpu
from jax.sharding import PartitionSpec as P

GROUPS = 32
FRAMES = 4
TH = 8
TW = 8
TILES = 4
HD = 128
N = 16
Z = 8
TOK = 256
LEN = N * TOK
C = 512
CO = C // N
HALF = CO // 2
TAPS = 27
PLANE = 9 * C
DEPTH = TAPS * C + 128
BQ = 512
BK = 512
EXTRA = 16
STEPS = LEN // BQ
PITCH = 24
BF = jnp.bfloat16
F32 = jnp.float32
MESH = pl.DeviceIdType.MESH
RIMS = ((1, 1, 0), (0, -1, 0), (3, 0, 1), (2, 0, -1), (1, 1, 1), (1, 1, -1), (0, -1, 1), (0, -1, -1))


def unit_kernel(
    q_ref, k_ref, v_ref, taps_ref, wp_ref, gain_ref, shift_ref, bias_ref, out_ref,
    q_raw, k_raw, v_raw, by_token, q_out, k_out, v_out,
    q_all, k_all, v_all, v_t, s_even, s_odd, m_buf, o_buf, att,
    w_all, lat, by_lanes, lat_t, edges, rims, stat, stats, field, x_t, out_t, gathered,
    q_send, q_recv, k_send, k_recv, v_send, v_recv, o_send, o_recv,
    raw_in, w_own, w_send, w_recv, c_send, c_recv, e_send, e_recv, t_send, t_recv, y_send, y_recv,
):
    me = lax.axis_index("seq")
    rep = lax.axis_index("rep")
    x_hi = rep // Z
    z = lax.rem(rep, Z)
    half = lax.rem(me, 2)
    other_core = me + 1 - 2 * half
    beside = {
        "seq": me + 2 - 4 * lax.rem(me // 2, 2),
        "rep": lax.rem(rep + Z, N),
    }

    barrier = pltpu.get_barrier_semaphore()

    def greet(t, carry):
        pl.semaphore_signal(
            barrier, inc=1, device_id={"seq": lax.rem(me + t, N)}, device_id_type=MESH
        )
        pl.semaphore_signal(
            barrier, inc=1, device_id={"rep": lax.rem(rep + t, N)}, device_id_type=MESH
        )
        return carry

    lax.fori_loop(1, N, greet, 0)
    pl.semaphore_signal(barrier, inc=1, device_id=beside, device_id_type=MESH)

    k_in = pltpu.make_async_copy(k_ref, k_raw, raw_in.at[0])
    v_in = pltpu.make_async_copy(v_ref, v_raw, raw_in.at[1])
    q_in = pltpu.make_async_copy(q_ref, q_raw, raw_in.at[2])
    k_in.start()
    v_in.start()
    q_in.start()

    def ds(start, size):
        return pl.ds(pl.multiple_of(start, size), size)

    def own_tap(t):
        return pltpu.make_async_copy(
            taps_ref.at[t], w_all.at[ds(rep * CO, CO), ds(t * C, C)], w_own.at[t]
        )

    def tap_start(t, carry):
        own_tap(t).start()
        return carry

    lax.fori_loop(0, TAPS, tap_start, 0)
    square = (CO, CO)
    on = lax.broadcasted_iota(jnp.int32, square, 0) == lax.broadcasted_iota(jnp.int32, square, 1)
    bias = jnp.sum(
        jnp.where(on, jnp.broadcast_to(bias_ref[...], square), 0.0), axis=1, keepdims=True
    )
    high = bias.astype(BF).astype(F32)
    middle = (bias - high).astype(BF).astype(F32)
    low = bias - high - middle
    lane = lax.broadcasted_iota(jnp.int32, (CO, HD), 1)
    nought = jnp.zeros((CO, HD), F32)
    parts = jnp.where(lane == 0, high, jnp.where(lane == 1, middle, jnp.where(lane == 2, low, nought)))
    w_all[ds(rep * CO, CO), TAPS * C :] = parts.astype(BF)
    v_t[HD:] = jnp.ones((EXTRA, LEN), BF)

    def by_head(copy, raw, out):
        copy.wait()

        def widen(b, carry):
            by_token[ds(b * TOK, TOK)] = raw[ds(b * TOK, TOK)].astype(F32)
            return carry

        lax.fori_loop(0, N, widen, 0)
        for h in range(N):
            out[h] = by_token[pl.ds(h, TOK, stride=N)].astype(BF)

    by_head(k_in, k_raw, k_out)
    pl.semaphore_wait(barrier, 2 * (N - 1) + 1)

    def k_copy(t):
        to = lax.rem(me + t, N)
        return pltpu.make_async_remote_copy(
            src_ref=k_out.at[to], dst_ref=k_all.at[ds(me * TOK, TOK), pl.ds(0, HD)],
            send_sem=k_send.at[t], recv_sem=k_recv.at[t],
            device_id={"seq": to}, device_id_type=MESH,
        )

    def v_copy(t):
        to = lax.rem(me + t, N)
        return pltpu.make_async_remote_copy(
            src_ref=v_out.at[to], dst_ref=v_all.at[ds(me * TOK, TOK)],
            send_sem=v_send.at[t], recv_sem=v_recv.at[t],
            device_id={"seq": to}, device_id_type=MESH,
        )

    def q_copy(t):
        to = lax.rem(me - t + N, N)
        return pltpu.make_async_remote_copy(
            src_ref=q_out.at[to], dst_ref=q_all.at[ds(t * TOK, TOK)],
            send_sem=q_send.at[t], recv_sem=q_recv.at[t],
            device_id={"seq": to}, device_id_type=MESH,
        )

    def o_copy(t):
        to = lax.rem(me + t, N)
        return pltpu.make_async_remote_copy(
            src_ref=o_buf.at[ds(t * TOK, TOK)], dst_ref=att.at[:, ds(me * HD, HD)],
            send_sem=o_send.at[t], recv_sem=o_recv.at[t],
            device_id={"seq": to}, device_id_type=MESH,
        )

    def every(act, copy, first=1, last=N):
        def body(t, carry):
            getattr(copy(t), act)()
            return carry
        lax.fori_loop(first, last, body, 0)

    pieces = (
        [(0, -d, "up") for d in (1, 2, 3, 4)] + [(0, d, "down") for d in (1, 2, 3)]
        + [(1, d, "across") for d in (0, -1, -2, -3, 3, 4)] + [(1, d, "down") for d in (1, 2)]
    )

    def shard_rows(x, d):
        at_x = 1 - x_hi if x else x_hi
        return ds((at_x * Z + lax.rem(z + d + Z, Z)) * CO + half * HALF, HALF)

    def w_copy(i):
        x, d, way = pieces[i]
        if way == "across":
            held, to = shard_rows(0, d), beside
        else:
            turn = 1 if way == "up" else -1
            held = shard_rows(x, d + turn)
            to = {"rep": x_hi * Z + lax.rem(z + turn + Z, Z)}
        return pltpu.make_async_remote_copy(
            src_ref=w_all.at[held], dst_ref=w_all.at[held],
            send_sem=w_send.at[i], recv_sem=w_recv.at[i],
            device_id=to, device_id_type=MESH,
        )

    def core_copy(i):
        x, d, _ = pieces[i]
        held = shard_rows(x, d)
        return pltpu.make_async_remote_copy(
            src_ref=w_all.at[held], dst_ref=w_all.at[held],
            send_sem=c_send.at[i], recv_sem=c_recv.at[i],
            device_id={"seq": other_core}, device_id_type=MESH,
        )

    def relay(i, *onward):
        w_copy(i).wait_recv()
        for j in onward:
            w_copy(j).start()
        core_copy(i).start()

    every("start", k_copy)
    every("wait", own_tap, 0, TAPS)
    w_copy(0).start()
    w_copy(4).start()
    w_copy(7).start()
    by_head(v_in, v_raw, v_out)
    every("start", v_copy)
    by_head(q_in, q_raw, q_out)
    every("start", q_copy)

    def twice(place, block):
        k_all[place, HD:] = block

    def flip(place, block):
        v_t[:HD, place] = jnp.transpose(block)

    mine = ds(me * TOK, TOK)
    k_all[mine, :HD] = k_out[me]
    twice(mine, k_out[me])
    flip(mine, v_out[me])
    q_all[:TOK] = q_out[me]

    def k_arrive(t, carry):
        k_copy(t).wait_recv()
        place = ds(lax.rem(me - t + N, N) * TOK, TOK)
        twice(place, k_all[place, :HD])
        return carry

    lax.fori_loop(1, N, k_arrive, 0)

    factor = HD ** (-0.5) * math.log2(math.e)

    def query_pair(u):
        wide = q_all[ds(u * BQ, BQ)].astype(F32) * factor
        first = wide.astype(BF)
        rest = (wide - first.astype(F32)).astype(BF)
        return jnp.concatenate([jnp.transpose(first), jnp.transpose(rest)], axis=0)

    def scores(pair, s_buf, c, top):
        keys = pl.ds(c * BK, BK)
        s = jnp.dot(k_all[keys], pair, preferred_element_type=F32)
        s_buf[keys] = s
        part = jnp.max(s.reshape(BK // 8, 8, BQ), axis=0)
        return part if top is None else jnp.maximum(top, part)

    def settle(top):
        m_buf[...] = jnp.broadcast_to(jnp.max(top, axis=0, keepdims=True), (8, BQ))

    def weigh(s_buf, c, m, total):
        keys = pl.ds(c * BK, BK)
        p = jnp.exp2(s_buf[keys].reshape(BK // 8, 8, BQ) - m[None]).reshape(BK, BQ).astype(BF)
        got = jnp.dot(v_t[:, keys], p, preferred_element_type=F32)
        return got if total is None else total + got

    def emit(u, total):
        o = (total[:HD] / total[HD : HD + 1]).astype(BF)
        o_buf[ds(u * BQ, BQ)] = jnp.transpose(o)

    def step(u, now, then):
        if then is not None:
            q_copy(2 * u + 2).wait_recv()
            q_copy(2 * u + 3).wait_recv()
            pair = query_pair(u + 1)
        m = m_buf[...]
        top = None
        total = None
        for c in range(LEN // BK):
            if then is not None:
                top = scores(pair, then, c, top)
            total = weigh(now, c, m, total)
        if then is not None:
            settle(top)
        emit(u, total)

    q_copy(1).wait_recv()
    pair = query_pair(0)
    top = None
    for c in range(LEN // BK):
        top = scores(pair, s_even, c, top)
    settle(top)
    relay(0, 1, 8)
    relay(4, 5)
    relay(7, 13)

    def v_arrive(t, carry):
        v_copy(t).wait_recv()
        place = ds(lax.rem(me - t + N, N) * TOK, TOK)
        flip(place, v_all[place])
        return carry

    lax.fori_loop(1, N, v_arrive, 0)
    relay(1, 2, 9)
    relay(5, 6)
    relay(8)

    def steps(i, carry):
        step(2 * i, s_even, s_odd)

        @pl.when(i > 0)
        def _():
            o_copy(4 * i).start()

        o_copy(4 * i + 1).start()

        step(2 * i + 1, s_odd, s_even)
        o_copy(4 * i + 2).start()
        o_copy(4 * i + 3).start()

        @pl.when(i == 0)
        def _():
            relay(2, 3, 10)
            relay(6, 11)
            relay(9)

        @pl.when(i == 1)
        def _():
            relay(3, 12)
            relay(13, 14)
            relay(10)

        @pl.when(i == 2)
        def _():
            relay(11)
            relay(14)

        return carry

    lax.fori_loop(0, STEPS // 2 - 1, steps, 0)
    step(STEPS - 2, s_even, s_odd)
    o_copy(N - 4).start()
    o_copy(N - 3).start()
    step(STEPS - 1, s_odd, None)
    o_copy(N - 2).start()
    o_copy(N - 1).start()
    own_o = pltpu.make_async_copy(o_buf.at[pl.ds(0, TOK)], att.at[:, ds(me * HD, HD)], o_recv.at[0])
    own_o.start()
    every("wait_send", k_copy)
    every("wait_send", v_copy)
    every("wait_send", q_copy)
    own_o.wait()
    every("wait_recv", o_copy)

    latent = jnp.dot(att[...], wp_ref[...], preferred_element_type=F32).astype(BF)
    wide = latent.astype(F32)
    lat[...] = wide
    for f in range(FRAMES):
        at = pl.ds(f * TW, TW)
        edges[0, at] = lat[pl.ds(f * TH * TW, TW)].astype(BF)
        edges[1, at] = lat[pl.ds((f + 1) * TH * TW - TW, TW)].astype(BF)
    for j in range(C // HD):
        lanes = pl.ds(j * HD, HD)
        by_lanes[j] = wide[:, j * HD : (j + 1) * HD]
        edges[2, :, lanes] = by_lanes[j, pl.ds(0, FRAMES * TH, stride=TW)].astype(BF)
        edges[3, :, lanes] = by_lanes[j, pl.ds(TW - 1, FRAMES * TH, stride=TW)].astype(BF)

    row, column = me // TILES, lax.rem(me, TILES)

    def rim_copy(n):
        edge, down, right = RIMS[n]
        to = lax.rem(row + down + TILES, TILES) * TILES + lax.rem(column + right + TILES, TILES)
        return pltpu.make_async_remote_copy(
            src_ref=edges.at[edge], dst_ref=rims.at[n],
            send_sem=e_send.at[n], recv_sem=e_recv.at[n],
            device_id={"seq": to}, device_id_type=MESH,
        )

    for n in range(len(RIMS)):
        rim_copy(n).start()

    line = lax.broadcasted_iota(jnp.int32, (8, C), 0)
    sums = jnp.where(
        line == 0,
        jnp.sum(wide, axis=0, keepdims=True),
        jnp.where(line == 1, jnp.sum(wide * wide, axis=0, keepdims=True), 0.0),
    )
    size = C // GROUPS
    member = lax.broadcasted_iota(jnp.int32, (C, HD), 0) // size
    into = (member == lax.broadcasted_iota(jnp.int32, (C, HD), 1)).astype(F32)
    stat[...] = jnp.dot(
        sums, into, precision=lax.Precision.HIGHEST, preferred_element_type=F32
    )

    def stat_copy(t):
        return pltpu.make_async_remote_copy(
            src_ref=stat, dst_ref=stats.at[me],
            send_sem=t_send.at[t], recv_sem=t_recv.at[t],
            device_id={"seq": lax.rem(me + t, N)}, device_id_type=MESH,
        )

    every("start", stat_copy)
    stats[me] = stat[...]
    lat_t[...] = jnp.transpose(latent)
    x_t[PLANE:] = jnp.where(
        lax.broadcasted_iota(jnp.int32, (128, TOK), 0) < 3, 1.0, 0.0
    ).astype(BF)
    every("wait_recv", stat_copy)

    total = jnp.sum(stats[...], axis=0) / (LEN * size)
    mean = total[0:1]
    var = total[1:2] - mean * mean
    pick = lax.broadcasted_iota(jnp.int32, (8, HD), 0)
    both = jnp.where(pick == 0, mean, jnp.where(pick == 1, lax.rsqrt(var + 1e-06), 0.0))
    member = lax.broadcasted_iota(jnp.int32, (HD, C), 1) // size
    out_of = (member == lax.broadcasted_iota(jnp.int32, (HD, C), 0)).astype(F32)
    both = jnp.dot(both, out_of, precision=lax.Precision.HIGHEST, preferred_element_type=F32)
    mean, inverse = both[0:1], both[1:2]
    gain, shift = gain_ref[...], shift_ref[...]

    def activate(x):
        return jax.nn.silu((x - mean) * inverse * gain + shift)

    inner = activate(lat[...])
    for f in range(FRAMES):
        for h in range(TH):
            place = (f * (TH + 2) + 1 + h) * PITCH + 8
            field[pl.ds(place, TW)] = inner[(f * TH + h) * TW : (f * TH + h + 1) * TW]

    above, below = row > 0, row < TILES - 1
    before, after = column > 0, column < TILES - 1
    inside = (
        above, below, before, after,
        above & before, above & after, below & before, below & after,
    )
    for n in range(len(RIMS)):
        rim_copy(n).wait_recv()
        rim = jnp.where(inside[n], activate(rims[n].astype(F32)), 0.0)
        for f in range(FRAMES):
            mine = rim[f * TW : (f + 1) * TW]
            first = f * (TH + 2) * PITCH
            last = first + (TH + 1) * PITCH
            if n == 0:
                field[pl.ds(first + 8, TW)] = mine
            elif n == 1:
                field[pl.ds(last + 8, TW)] = mine
            elif n == 2:
                for h in range(TH):
                    field[pl.ds(first + (h + 1) * PITCH + 7, 1)] = mine[h : h + 1]
            elif n == 3:
                for h in range(TH):
                    field[pl.ds(first + (h + 1) * PITCH + 16, 1)] = mine[h : h + 1]
            elif n == 4:
                field[pl.ds(first + 7, 1)] = mine[TW - 1 :]
            elif n == 5:
                field[pl.ds(first + 16, 1)] = mine[:1]
            elif n == 6:
                field[pl.ds(last + 7, 1)] = mine[TW - 1 :]
            else:
                field[pl.ds(last + 16, 1)] = mine[:1]

    for r in range(3):
        for s in range(3):
            window = jnp.concatenate(
                [
                    field[pl.ds((f * (TH + 2) + r + h) * PITCH + 7 + s, TW)]
                    for f in range(FRAMES)
                    for h in range(TH)
                ],
                axis=0,
            )
            x_t[pl.ds((r * 3 + s) * C, C)] = jnp.transpose(window.astype(BF))

    relay(12)
    every_piece = range(len(pieces))
    for i in every_piece:
        core_copy(i).wait_recv()

    now = jnp.dot(w_all[:, 2 * PLANE :], x_t[...], preferred_element_type=F32)
    one = jnp.dot(w_all[:, PLANE : 2 * PLANE], x_t[:PLANE], preferred_element_type=F32)
    two = jnp.dot(w_all[:, :PLANE], x_t[:PLANE, : TOK // 2], preferred_element_type=F32)
    at = lax.broadcasted_iota(jnp.int32, (C, TOK), 1)
    frame = TH * TW
    one = jnp.where(at >= frame, pltpu.roll(one, frame, 1), 0.0)
    two = jnp.concatenate([jnp.zeros((C, TOK // 2), F32), two], axis=1)
    out_t[...] = (lat_t[...].astype(F32) + now + one + two).astype(BF)

    def y_copy(t):
        to = lax.rem(rep + t, N)
        return pltpu.make_async_remote_copy(
            src_ref=out_t.at[ds(to * CO, CO)], dst_ref=gathered.at[rep],
            send_sem=y_send.at[t], recv_sem=y_recv.at[t],
            device_id={"rep": to}, device_id_type=MESH,
        )

    every("start", y_copy)
    gathered[rep] = out_t[ds(rep * CO, CO)]
    for i in every_piece:
        w_copy(i).wait_send()
        core_copy(i).wait_send()
    for n in range(len(RIMS)):
        rim_copy(n).wait_send()
    every("wait_send", o_copy)
    every("wait_send", stat_copy)
    every("wait_recv", y_copy)
    out_ref[...] = gathered[...]
    every("wait_send", y_copy)


def unit(q, k, v, taps, w_proj, gain, shift, bias):
    sem = pltpu.SemaphoreType.DMA
    vmem = pl.BlockSpec(memory_space=pltpu.VMEM)
    return pl.pallas_call(
        unit_kernel,
        out_shape=jax.ShapeDtypeStruct((N, CO, TOK), BF),
        in_specs=[pl.BlockSpec(memory_space=pl.ANY)] * 4 + [vmem] * 4,
        out_specs=vmem,
        scratch_shapes=[
            pltpu.VMEM((LEN, HD), BF),
            pltpu.VMEM((LEN, HD), BF),
            pltpu.VMEM((LEN, HD), BF),
            pltpu.VMEM((LEN, HD), F32),
            pltpu.VMEM((N, TOK, HD), BF),
            pltpu.VMEM((N, TOK, HD), BF),
            pltpu.VMEM((N, TOK, HD), BF),
            pltpu.VMEM((LEN, HD), BF),
            pltpu.VMEM((LEN, 2 * HD), BF),
            pltpu.VMEM((LEN, HD), BF),
            pltpu.VMEM((HD + EXTRA, LEN), BF),
            pltpu.VMEM((LEN, BQ), F32),
            pltpu.VMEM((LEN, BQ), F32),
            pltpu.VMEM((8, BQ), F32),
            pltpu.VMEM((LEN, HD), BF),
            pltpu.VMEM((TOK, N * HD), BF),
            pltpu.VMEM((C, DEPTH), BF),
            pltpu.VMEM((TOK, C), F32),
            pltpu.VMEM((C // HD, TOK, HD), F32),
            pltpu.VMEM((C, TOK), BF),
            pltpu.VMEM((4, FRAMES * TW, C), BF),
            pltpu.VMEM((len(RIMS), FRAMES * TW, C), BF),
            pltpu.VMEM((8, HD), F32),
            pltpu.VMEM((N, 8, HD), F32),
            pltpu.VMEM((FRAMES * (TH + 2) * PITCH, C), F32),
            pltpu.VMEM((PLANE + 128, TOK), BF),
            pltpu.VMEM((C, TOK), BF),
            pltpu.VMEM((N, CO, TOK), BF),
        ]
        + [sem((N,))] * 8
        + [sem((3,)), sem((TAPS,))]
        + [sem((N,))] * 4
        + [sem((len(RIMS),))] * 2
        + [sem((N,))] * 4,
        compiler_params=pltpu.CompilerParams(
            collective_id=0, has_side_effects=True, vmem_limit_bytes=62 * 2**20
        ),
        cost_estimate=pl.CostEstimate(
            flops=4 * LEN * LEN * HD + 2 * TOK * DEPTH * C,
            bytes_accessed=8 * 2**20,
            transcendentals=LEN * LEN,
        ),
        name="unit",
    )(q, k, v, taps, w_proj, gain, shift, bias)


def shards(queries, keys, values, w_proj, norm_gain, norm_bias, conv_weight, conv_bias):
    taps = conv_weight.reshape(TAPS, C, CO).transpose(0, 2, 1)
    q, k, v = (a.reshape(LEN, HD) for a in (queries, keys, values))
    out = unit(
        q, k, v, taps, w_proj, norm_gain[None], norm_bias[None], conv_bias[None]
    )
    return out.transpose(0, 2, 1).reshape(N, 1, FRAMES, TH, TW, CO)


def solution(mesh):
    return jax.shard_map(
        shards,
        mesh=mesh,
        in_specs=(
            P("rep", "seq", None, None),
            P("rep", "seq", None, None),
            P("rep", "seq", None, None),
            P(),
            P(),
            P(),
            P(None, None, None, None, "rep"),
            P("rep"),
        ),
        out_specs=P(None, "seq", None, None, None, "rep"),
        check_vma=False,
    )
```

```python
import math

import jax
import jax.numpy as jnp
from jax import lax
from jax.experimental import pallas as pl
from jax.experimental.pallas import tpu as pltpu
from jax.sharding import PartitionSpec as P

GROUPS = 32
FRAMES = 4
TH = 8
TW = 8
TILES = 4
HD = 128
N = 16
Z = 8
TOK = 256
LEN = N * TOK
C = 512
CO = C // N
HALF = CO // 2
TAPS = 27
PLANE = 9 * C
DEPTH = TAPS * C + 128
BQ = 512
BK = 512
EXTRA = 16
STEPS = LEN // BQ
PITCH = 24
BF = jnp.bfloat16
F32 = jnp.float32
MESH = pl.DeviceIdType.MESH
CORNERS = 4 * FRAMES * TW
RIMS = (
    (32, 32, 1, 0), (0, 32, -1, 0), (96, 32, 0, 1), (64, 32, 0, -1),
    (CORNERS + 48, 16, 1, 1), (CORNERS + 32, 16, 1, -1), (CORNERS + 16, 16, -1, 1), (CORNERS, 16, -1, -1),
)
RIM_ROWS = CORNERS + 4 * 16
CH = C // 2


def unit_kernel(
    q_ref, k_ref, v_ref, taps_ref, wp_ref, gain_ref, shift_ref, bias_ref, out_ref,
    q_raw, k_raw, v_raw, by_token, q_out, k_out, v_out,
    k_stop, v_stop, q_all, k_all, v_all, v_t, s_even, s_odd, m_buf, q_t, acc, o_buf, att, wp,
    w_all, lat, by_lanes, edges, rims, stat, stats, moments, field, x_t, by_frame, out_t, gathered,
    q_send, q_recv, k_send, k_recv, v_send, v_recv, o_send, o_recv,
    k_stop_send, k_stop_recv, v_stop_send, v_stop_recv,
    raw_in, w_own, w_send, w_recv, c_send, c_recv, e_send, e_recv, t_send, t_recv, b_send, b_recv, y_send, y_recv,
):
    me = lax.axis_index("seq")
    rep = lax.axis_index("rep")
    x_hi = rep // Z
    z = lax.rem(rep, Z)
    half = lax.rem(me, 2)
    other_core = me + 1 - 2 * half
    twin = me + 2 - 4 * lax.rem(me // 2, 2)
    beside = {"seq": twin, "rep": lax.rem(rep + Z, N)}

    def along_z(d):
        return x_hi * Z + lax.rem(z + d + Z, Z)

    barrier = pltpu.get_barrier_semaphore()

    def greet(t, carry):
        pl.semaphore_signal(
            barrier, inc=1, device_id={"seq": lax.rem(me + t, N)}, device_id_type=MESH
        )
        return carry

    def greet_z(t, carry):
        for seq in (me, twin):
            pl.semaphore_signal(
                barrier, inc=1, device_id={"seq": seq, "rep": along_z(t)}, device_id_type=MESH
            )
        return carry

    lax.fori_loop(1, N, greet, 0)
    lax.fori_loop(1, Z, greet_z, 0)
    pl.semaphore_signal(barrier, inc=1, device_id=beside, device_id_type=MESH)

    k_in = pltpu.make_async_copy(k_ref, k_raw, raw_in.at[0])
    v_in = pltpu.make_async_copy(v_ref, v_raw, raw_in.at[1])
    q_in = pltpu.make_async_copy(q_ref, q_raw, raw_in.at[2])
    wp_in = pltpu.make_async_copy(wp_ref, wp, raw_in.at[3])
    k_in.start()
    v_in.start()
    q_in.start()
    wp_in.start()

    def ds(start, size):
        return pl.ds(pl.multiple_of(start, size), size)

    def own_tap(t):
        return pltpu.make_async_copy(
            taps_ref.at[t], w_all.at[ds(z * CO, CO), ds(t * C, C)], w_own.at[t]
        )

    def tap_start(t, carry):
        own_tap(t).start()
        return carry

    lax.fori_loop(0, TAPS, tap_start, 0)
    square = (CO, CO)
    on = lax.broadcasted_iota(jnp.int32, square, 0) == lax.broadcasted_iota(jnp.int32, square, 1)
    bias = jnp.sum(
        jnp.where(on, jnp.broadcast_to(bias_ref[...], square), 0.0), axis=1, keepdims=True
    )
    high = bias.astype(BF).astype(F32)
    middle = (bias - high).astype(BF).astype(F32)
    low = bias - high - middle
    lane = lax.broadcasted_iota(jnp.int32, (CO, HD), 1)
    nought = jnp.zeros((CO, HD), F32)
    parts = jnp.where(lane == 0, high, jnp.where(lane == 1, middle, jnp.where(lane == 2, low, nought)))
    w_all[ds(z * CO, CO), TAPS * C :] = parts.astype(BF)
    v_t[HD:] = jnp.ones((EXTRA, LEN), BF)

    def by_head(copy, raw, out):
        copy.wait()

        def widen(b, carry):
            by_token[ds(b * TOK, TOK)] = raw[ds(b * TOK, TOK)].astype(F32)
            return carry

        lax.fori_loop(0, N, widen, 0)
        for h in range(N):
            out[h] = by_token[pl.ds(h, TOK, stride=N)].astype(BF)

    by_head(k_in, k_raw, k_out)
    pl.semaphore_wait(barrier, N + 2 * (Z - 1))

    band, lo = me // TILES, lax.rem(me // 2, 2)

    def column_of(j):
        return 2 * (lo + j // 2 - 2 * lo * (j // 2)) + half + j % 2 - 2 * half * (j % 2)

    def across_rows(j, rows):
        way = -1 if j < 2 else 1
        return lax.rem(band + way * rows + TILES, TILES) * TILES

    def straight(t):
        row = lax.rem(me + t, N) // TILES
        return lax.rem(row - band + TILES, TILES) != 2

    class Exchange:
        def __init__(self, out, whole, send, recv, stop, stop_send, stop_recv):
            self.out, self.whole, self.send, self.recv = out, whole, send, recv
            self.stop, self.stop_send, self.stop_recv = stop, stop_send, stop_recv

        def copy(self, t):
            to = lax.rem(me + t, N)
            return pltpu.make_async_remote_copy(
                src_ref=self.out.at[to], dst_ref=self.whole.at[ds(me * TOK, TOK)],
                send_sem=self.send.at[t], recv_sem=self.recv.at[t],
                device_id={"seq": to}, device_id_type=MESH,
            )

        def first(self, j):
            to = across_rows(j, 2) + column_of(j)
            t = lax.rem(to - me + N, N)
            return pltpu.make_async_remote_copy(
                src_ref=self.out.at[to], dst_ref=self.stop.at[j],
                send_sem=self.send.at[t], recv_sem=self.stop_recv.at[j],
                device_id={"seq": across_rows(j, 1) + lax.rem(me, TILES)}, device_id_type=MESH,
            )

        def second(self, j):
            to = across_rows(j, 1) + column_of(j)
            origin = across_rows(j, -1) + lax.rem(me, TILES)
            t = lax.rem(to - origin + N, N)
            return pltpu.make_async_remote_copy(
                src_ref=self.stop.at[j], dst_ref=self.whole.at[ds(origin * TOK, TOK)],
                send_sem=self.stop_send.at[j], recv_sem=self.recv.at[t],
                device_id={"seq": to}, device_id_type=MESH,
            )

        def start(self):
            for j in range(4):
                self.first(j).start()

            def body(t, carry):
                @pl.when(straight(t))
                def _():
                    self.copy(t).start()
                return carry

            lax.fori_loop(1, N, body, 0)

        def forward(self):
            for j in range(4):
                self.first(j).wait_recv()
                self.second(j).start()

        def wait_send(self):
            every("wait_send", self.copy)
            for j in range(4):
                self.second(j).wait_send()

    def q_copy(t):
        to = lax.rem(me - t + N, N)
        return pltpu.make_async_remote_copy(
            src_ref=q_out.at[to], dst_ref=q_all.at[ds(t * TOK, TOK)],
            send_sem=q_send.at[t], recv_sem=q_recv.at[t],
            device_id={"seq": to}, device_id_type=MESH,
        )

    def o_copy(t):
        to = lax.rem(me + t, N)
        return pltpu.make_async_remote_copy(
            src_ref=o_buf.at[ds(t * TOK, TOK)], dst_ref=att.at[:, ds(me * HD, HD)],
            send_sem=o_send.at[t], recv_sem=o_recv.at[t],
            device_id={"seq": to}, device_id_type=MESH,
        )

    def every(act, copy, first=1, last=N):
        def body(t, carry):
            getattr(copy(t), act)()
            return carry
        lax.fori_loop(first, last, body, 0)

    k_move = Exchange(k_out, k_all, k_send, k_recv, k_stop, k_stop_send, k_stop_recv)
    v_move = Exchange(v_out, v_all, v_send, v_recv, v_stop, v_stop_send, v_stop_recv)

    pieces = [(-d, 1) for d in (1, 2, 3, 4)] + [(d, -1) for d in (1, 2, 3)]

    def shard_rows(d):
        return ds(lax.rem(z + d + Z, Z) * CO + half * HALF, HALF)

    def w_copy(i):
        d, turn = pieces[i]
        held = shard_rows(d + turn)
        return pltpu.make_async_remote_copy(
            src_ref=w_all.at[held], dst_ref=w_all.at[held],
            send_sem=w_send.at[i], recv_sem=w_recv.at[i],
            device_id={"rep": along_z(turn)}, device_id_type=MESH,
        )

    def core_copy(i):
        held = shard_rows(pieces[i][0])
        return pltpu.make_async_remote_copy(
            src_ref=w_all.at[held], dst_ref=w_all.at[held],
            send_sem=c_send.at[i], recv_sem=c_recv.at[i],
            device_id={"seq": other_core}, device_id_type=MESH,
        )

    def relay(i, *onward):
        w_copy(i).wait_recv()
        for j in onward:
            w_copy(j).start()
        core_copy(i).start()

    k_move.start()
    every("wait", own_tap, 0, TAPS)
    w_copy(0).start()
    w_copy(4).start()
    by_head(v_in, v_raw, v_out)
    by_head(q_in, q_raw, q_out)
    k_move.forward()

    def flip(place, block):
        v_t[:HD, place] = jnp.transpose(block)

    mine = ds(me * TOK, TOK)
    k_all[mine] = k_out[me]
    flip(mine, v_out[me])
    q_all[:TOK] = q_out[me]
    every("wait_recv", k_move.copy)
    v_move.start()
    every("start", q_copy, 1, 4)

    factor = HD ** (-0.5) * math.log2(math.e)

    def query_block(u):
        q_t[...] = jnp.transpose(q_all[ds(u * BQ, BQ)])

    def scores(s_buf, keys, top):
        s = jnp.dot(k_all[keys], q_t[...], preferred_element_type=F32)
        s_buf[keys] = s
        return jnp.maximum(top, jnp.max(s.reshape(BK // 8, 8, BQ), axis=0))

    lowest = jnp.full((8, BQ), -jnp.inf, F32)

    def settle(top):
        m_buf[...] = jnp.broadcast_to(jnp.max(top, axis=0, keepdims=True), (8, BQ))

    def exps(s_buf, keys, m):
        below = s_buf[keys].reshape(BK // 8, 8, BQ) - m[None]
        return jnp.exp2(below * factor).reshape(BK, BQ).astype(BF)

    def weigh(p, keys):
        acc[...] += jnp.dot(v_t[:, keys], p, preferred_element_type=F32)

    def emit(u):
        o = (acc[:HD] / acc[HD : HD + 1]).astype(BF)
        o_buf[ds(u * BQ, BQ)] = jnp.transpose(o)

    def step(u, now, then):
        if then is not None:
            q_copy(2 * u + 2).wait_recv()
            q_copy(2 * u + 3).wait_recv()
            query_block(u + 1)
        m = m_buf[...]
        acc[...] = jnp.zeros_like(acc)

        def chunk(c, top):
            keys = ds(c * BK, BK)
            p = exps(now, keys, m)
            if then is not None:
                top = scores(then, keys, top)
            weigh(p, keys)
            return top

        top = lax.fori_loop(0, LEN // BK, chunk, lowest)
        if then is not None:
            settle(top)
        emit(u)

    q_copy(1).wait_recv()
    query_block(0)
    settle(
        lax.fori_loop(
            0, LEN // BK, lambda c, top: scores(s_even, ds(c * BK, BK), top), lowest
        )
    )
    v_move.forward()
    relay(0, 1)
    relay(4, 5)

    def v_arrive(t, carry):
        v_move.copy(t).wait_recv()
        place = ds(lax.rem(me - t + N, N) * TOK, TOK)
        flip(place, v_all[place])
        return carry

    lax.fori_loop(1, N, v_arrive, 0)
    every("start", q_copy, 4, 8)
    relay(1, 2)
    relay(5, 6)

    def steps(i, carry):
        @pl.when(i < 2)
        def _():
            every("start", q_copy, 8 + 4 * i, 12 + 4 * i)

        step(2 * i, s_even, s_odd)

        @pl.when(i > 0)
        def _():
            o_copy(4 * i).start()

        o_copy(4 * i + 1).start()

        step(2 * i + 1, s_odd, s_even)
        o_copy(4 * i + 2).start()
        o_copy(4 * i + 3).start()

        @pl.when(i == 1)
        def _():
            relay(2, 3)
            relay(6)

        return carry

    lax.fori_loop(0, STEPS // 2 - 1, steps, 0)
    step(STEPS - 2, s_even, s_odd)
    o_copy(N - 4).start()
    o_copy(N - 3).start()
    step(STEPS - 1, s_odd, None)
    o_copy(N - 2).start()
    o_copy(N - 1).start()
    own_o = pltpu.make_async_copy(o_buf.at[pl.ds(0, TOK)], att.at[:, ds(me * HD, HD)], o_recv.at[0])
    own_o.start()
    relay(3)
    k_move.wait_send()
    v_move.wait_send()
    every("wait_send", q_copy)
    own_o.wait()
    every("wait_recv", o_copy)

    wp_in.wait()
    latent = jnp.dot(att[...], wp[...], preferred_element_type=F32).astype(BF)
    wide = latent.astype(F32)
    lat[0] = latent
    lat_copy = pltpu.make_async_remote_copy(
        src_ref=lat.at[0], dst_ref=lat.at[1], send_sem=b_send.at[0], recv_sem=b_recv.at[0],
        device_id=beside, device_id_type=MESH,
    )
    lat_copy.start()
    for f in range(FRAMES):
        first, last = f * TH * TW, (f + 1) * TH * TW - TW
        edges[pl.ds(f * TW, TW)] = wide[first : first + TW].astype(BF)
        edges[pl.ds((FRAMES + f) * TW, TW)] = wide[last : last + TW].astype(BF)
    for j in range(C // HD):
        lanes = pl.ds(j * HD, HD)
        by_lanes[j] = wide[:, j * HD : (j + 1) * HD]
        edges[pl.ds(64, 32), lanes] = by_lanes[j, pl.ds(0, FRAMES * TH, stride=TW)].astype(BF)
        edges[pl.ds(96, 32), lanes] = by_lanes[j, pl.ds(TW - 1, FRAMES * TH, stride=TW)].astype(BF)
        for n, start in enumerate((0, TW - 1, TW, 2 * TW - 1)):
            corner = by_lanes[j, pl.ds(start, 16, stride=2 * TW)]
            edges[pl.ds(CORNERS + 16 * n, 16), lanes] = corner.astype(BF)

    row, column = me // TILES, lax.rem(me, TILES)

    def rim_rows(n):
        return pl.ds(n * 32, 32) if n < 4 else pl.ds(CORNERS + (n - 4) * 16, 16)

    def rim_copy(n):
        at, size, down, right = RIMS[n]
        to = lax.rem(row + down + TILES, TILES) * TILES + lax.rem(column + right + TILES, TILES)
        return pltpu.make_async_remote_copy(
            src_ref=edges.at[pl.ds(at, size)], dst_ref=rims.at[0, rim_rows(n)],
            send_sem=e_send.at[n], recv_sem=e_recv.at[n],
            device_id={"seq": to}, device_id_type=MESH,
        )

    line = lax.broadcasted_iota(jnp.int32, (8, C), 0)
    stat[...] = jnp.where(
        line == 0,
        jnp.sum(wide, axis=0, keepdims=True),
        jnp.where(line == 1, jnp.sum(wide * wide, axis=0, keepdims=True), 0.0),
    )

    def stat_copy(t):
        return pltpu.make_async_remote_copy(
            src_ref=stat, dst_ref=stats.at[me],
            send_sem=t_send.at[t], recv_sem=t_recv.at[t],
            device_id={"seq": lax.rem(me + t, N)}, device_id_type=MESH,
        )

    every("start", stat_copy)
    for n in range(len(RIMS)):
        rim_copy(n).start()
    stats[me] = stat[...]
    x_t[PLANE:] = jnp.where(
        lax.broadcasted_iota(jnp.int32, (128, TOK), 0) < 3, 1.0, 0.0
    ).astype(BF)
    gain, shift = gain_ref[...], shift_ref[...]
    every("wait_recv", stat_copy)

    size = C // GROUPS
    total = jnp.sum(stats[...], axis=0)
    lane = lax.broadcasted_iota(jnp.int32, (8, C), 1)
    for hop in (1, 2, 4, 8):
        after = pltpu.roll(total, C - hop, 1)
        before = pltpu.roll(total, hop, 1)
        total = total + jnp.where(lax.rem(lane // hop, 2) == 0, after, before)
    total = total / (LEN * size)
    mean = total[0:1]
    var = total[1:2] - mean * mean
    moments[0] = jnp.where(line == 0, mean, jnp.where(line == 1, lax.rsqrt(var + 1e-06), 0.0))

    def to_beside(n, ref):
        return pltpu.make_async_remote_copy(
            src_ref=ref.at[0], dst_ref=ref.at[1], send_sem=b_send.at[n], recv_sem=b_recv.at[n],
            device_id=beside, device_id_type=MESH,
        )

    moments_copy = to_beside(1, moments)
    rims_copy = to_beside(2, rims)
    moments_copy.start()
    for n in range(len(RIMS)):
        rim_copy(n).wait_recv()
    rims_copy.start()

    def decode(which, tile):
        mean, inverse = moments[which, 0:1], moments[which, 1:2]

        def activate(x):
            return jax.nn.silu((x.astype(F32) - mean) * inverse * gain + shift)

        inner = activate(lat[which])
        for f in range(FRAMES):
            for h in range(TH):
                field[f * (TH + 2) + 1 + h, pl.ds(8, TW)] = inner[
                    (f * TH + h) * TW : (f * TH + h + 1) * TW
                ]

        row, column = tile // TILES, lax.rem(tile, TILES)
        above, below = row > 0, row < TILES - 1
        before, after = column > 0, column < TILES - 1
        inside = (
            above, below, before, after,
            above & before, above & after, below & before, below & after,
        )
        for n in range(len(RIMS)):
            rim = jnp.where(inside[n], activate(rims[which, rim_rows(n)]), 0.0)
            for f in range(FRAMES):
                first = f * (TH + 2)
                last = first + TH + 1
                if n < 2:
                    field[last if n else first, pl.ds(8, TW)] = rim[f * TW : (f + 1) * TW]
                elif n < 4:
                    for h in range(TH):
                        k = f * TH + h
                        field[first + h + 1, pl.ds(7 if n == 2 else 16, 1)] = rim[k : k + 1]
                else:
                    k = 4 * f + (3 if n < 6 else 0)
                    side = 7 if n in (4, 6) else 16
                    field[first if n < 6 else last, pl.ds(side, 1)] = rim[k : k + 1]

        def windows(r, carry):
            for s in range(3):
                window = jnp.concatenate(
                    [
                        field[r + (f * (TH + 2) + h), pl.ds(7 + s, TW)]
                        for f in range(FRAMES)
                        for h in range(TH)
                    ],
                    axis=0,
                )
                x_t[ds((r * 3 + s) * C, C)] = jnp.transpose(window.astype(BF))
            return carry

        lax.fori_loop(0, 3, windows, 0)
        if which == 0:
            for i in range(len(pieces)):
                core_copy(i).wait_recv()
        by_frame[2] = jnp.transpose(lat[which, :, ds(x_hi * CH, CH)]).astype(F32) + jnp.dot(
            w_all[:, TAPS * C :], x_t[PLANE:], preferred_element_type=F32
        )
        by_frame[:2] = jnp.zeros((2, CH, TOK), F32)

        def convolve(k, carry):
            x = x_t[ds(k * C, C)]
            for p in range(3):
                by_frame[p] += jnp.dot(
                    w_all[:, pl.ds(pl.multiple_of(p * PLANE + k * C, C), C)], x,
                    preferred_element_type=F32,
                )
            return carry

        lax.fori_loop(0, 9, convolve, 0)
        at = lax.broadcasted_iota(jnp.int32, (CH, TOK), 1)
        frame = TH * TW
        one = jnp.where(at >= frame, pltpu.roll(by_frame[1], frame, 1), 0.0)
        two = jnp.where(at >= 2 * frame, pltpu.roll(by_frame[0], 2 * frame, 1), 0.0)
        out_t[which] = (by_frame[2] + one + two).astype(BF)

    def y_copy(t):
        theirs, hop = t // Z, lax.rem(t, Z)
        video = lax.rem(rep + theirs * Z, N)
        return pltpu.make_async_remote_copy(
            src_ref=out_t.at[theirs, ds(lax.rem(z + hop, Z) * CO, CO)], dst_ref=gathered.at[video],
            send_sem=y_send.at[t], recv_sem=y_recv.at[t],
            device_id={"seq": me + theirs * (twin - me), "rep": along_z(hop)},
            device_id_type=MESH,
        )

    decode(0, me)
    every("start", y_copy, 1, Z)
    gathered[rep] = out_t[0, ds(z * CO, CO)]
    lat_copy.wait_recv()
    moments_copy.wait_recv()
    rims_copy.wait_recv()
    decode(1, twin)
    every("start", y_copy, Z, N)
    for i in range(len(pieces)):
        w_copy(i).wait_send()
        core_copy(i).wait_send()
    for n in range(len(RIMS)):
        rim_copy(n).wait_send()
    lat_copy.wait_send()
    moments_copy.wait_send()
    rims_copy.wait_send()
    every("wait_send", o_copy)
    every("wait_send", stat_copy)
    every("wait_recv", y_copy)
    out_ref[...] = gathered[...]
    every("wait_send", y_copy)


def unit(q, k, v, taps, w_proj, gain, shift, bias):
    sem = pltpu.SemaphoreType.DMA
    vmem = pl.BlockSpec(memory_space=pltpu.VMEM)
    return pl.pallas_call(
        unit_kernel,
        out_shape=jax.ShapeDtypeStruct((N, CO, TOK), BF),
        in_specs=[pl.BlockSpec(memory_space=pl.ANY)] * 5 + [vmem] * 3,
        out_specs=vmem,
        scratch_shapes=[
            pltpu.VMEM((LEN, HD), BF),
            pltpu.VMEM((LEN, HD), BF),
            pltpu.VMEM((LEN, HD), BF),
            pltpu.VMEM((LEN, HD), F32),
            pltpu.VMEM((N, TOK, HD), BF),
            pltpu.VMEM((N, TOK, HD), BF),
            pltpu.VMEM((N, TOK, HD), BF),
            pltpu.VMEM((4, TOK, HD), BF),
            pltpu.VMEM((4, TOK, HD), BF),
            pltpu.VMEM((LEN, HD), BF),
            pltpu.VMEM((LEN, HD), BF),
            pltpu.VMEM((LEN, HD), BF),
            pltpu.VMEM((HD + EXTRA, LEN), BF),
            pltpu.VMEM((LEN, BQ), F32),
            pltpu.VMEM((LEN, BQ), F32),
            pltpu.VMEM((8, BQ), F32),
            pltpu.VMEM((HD, BQ), BF),
            pltpu.VMEM((HD + EXTRA, BQ), F32),
            pltpu.VMEM((LEN, HD), BF),
            pltpu.VMEM((TOK, N * HD), BF),
            pltpu.VMEM((N * HD, C), BF),
            pltpu.VMEM((CH, DEPTH), BF),
            pltpu.VMEM((2, TOK, C), BF),
            pltpu.VMEM((C // HD, TOK, HD), F32),
            pltpu.VMEM((RIM_ROWS, C), BF),
            pltpu.VMEM((2, RIM_ROWS, C), BF),
            pltpu.VMEM((8, C), F32),
            pltpu.VMEM((N, 8, C), F32),
            pltpu.VMEM((2, 8, C), F32),
            pltpu.VMEM((FRAMES * (TH + 2), PITCH, C), F32),
            pltpu.VMEM((PLANE + 128, TOK), BF),
            pltpu.VMEM((3, CH, TOK), F32),
            pltpu.VMEM((2, CH, TOK), BF),
            pltpu.VMEM((N, CO, TOK), BF),
        ]
        + [sem((N,))] * 8
        + [sem((4,))] * 4
        + [sem((4,)), sem((TAPS,))]
        + [sem((7,))] * 4
        + [sem((len(RIMS),))] * 2
        + [sem((N,))] * 2
        + [sem((3,))] * 2
        + [sem((N,))] * 2,
        compiler_params=pltpu.CompilerParams(
            collective_id=0, has_side_effects=True, vmem_limit_bytes=62 * 2**20
        ),
        cost_estimate=pl.CostEstimate(
            flops=4 * LEN * LEN * HD + 2 * TOK * DEPTH * C,
            bytes_accessed=8 * 2**20,
            transcendentals=LEN * LEN,
        ),
        name="unit",
    )(q, k, v, taps, w_proj, gain, shift, bias)


def shards(queries, keys, values, w_proj, norm_gain, norm_bias, conv_weight, conv_bias):
    taps = conv_weight.reshape(TAPS, C, CO).transpose(0, 2, 1)
    q, k, v = (a.reshape(LEN, HD) for a in (queries, keys, values))
    out = unit(
        q, k, v, taps, w_proj, norm_gain[None], norm_bias[None], conv_bias[None]
    )
    return out.transpose(0, 2, 1).reshape(N, 1, FRAMES, TH, TW, CO)


def solution(mesh):
    return jax.shard_map(
        shards,
        mesh=mesh,
        in_specs=(
            P("rep", "seq", None, None),
            P("rep", "seq", None, None),
            P("rep", "seq", None, None),
            P(),
            P(),
            P(),
            P(None, None, None, None, "rep"),
            P("rep"),
        ),
        out_specs=P(None, "seq", None, None, None, "rep"),
        check_vma=False,
    )
```

```python
import math

import jax
import jax.numpy as jnp
from jax import lax
from jax.experimental import pallas as pl
from jax.experimental.pallas import tpu as pltpu
from jax.sharding import PartitionSpec as P

GROUPS = 32
FRAMES = 4
TH = 8
TW = 8
TILES = 4
HD = 128
N = 16
Z = 8
TOK = 256
LEN = N * TOK
C = 512
CO = C // N
HALF = CO // 2
TAPS = 27
PLANE = 9 * C
BQ = 512
BK = 512
EXTRA = 16
STEPS = LEN // BQ
PITCH = 24
BF = jnp.bfloat16
F32 = jnp.float32
MESH = pl.DeviceIdType.MESH
CORNERS = 4 * FRAMES * TW
RIMS = (
    (32, 32, 1, 0), (0, 32, -1, 0), (96, 32, 0, 1), (64, 32, 0, -1),
    (CORNERS + 48, 16, 1, 1), (CORNERS + 32, 16, 1, -1), (CORNERS + 16, 16, -1, 1), (CORNERS, 16, -1, -1),
)
RIM_ROWS = CORNERS + 4 * 16
CH = C // 2


def unit_kernel(
    q_ref, k_ref, v_ref, taps_ref, wp_ref, gain_ref, shift_ref, bias_ref, out_ref,
    q_raw, k_raw, v_raw, by_token, q_out, k_out, v_out,
    q_all, k_all, v_all, v_t, s_even, s_odd, m_buf, q_t, acc, o_buf, att, wp,
    w_all, lat, by_lanes, edges, rims, stat, stats, moments, field, ones, by_frame, out_t, gathered,
    q_send, q_recv, k_send, k_recv, v_send, v_recv, o_send, o_recv,
    raw_in, w_own, w_send, w_recv, c_send, c_recv, e_send, e_recv, t_send, t_recv, b_send, b_recv, y_send, y_recv,
):
    me = lax.axis_index("seq")
    rep = lax.axis_index("rep")
    x_hi = rep // Z
    z = lax.rem(rep, Z)
    half = lax.rem(me, 2)
    other_core = me + 1 - 2 * half
    twin = me + 2 - 4 * lax.rem(me // 2, 2)
    beside = {"seq": twin, "rep": lax.rem(rep + Z, N)}

    def along_z(d):
        return x_hi * Z + lax.rem(z + d + Z, Z)

    barrier = pltpu.get_barrier_semaphore()

    def greet(t, carry):
        pl.semaphore_signal(
            barrier, inc=1, device_id={"seq": lax.rem(me + t, N)}, device_id_type=MESH
        )
        return carry

    def greet_z(t, carry):
        for seq in (me, twin):
            pl.semaphore_signal(
                barrier, inc=1, device_id={"seq": seq, "rep": along_z(t)}, device_id_type=MESH
            )
        return carry

    lax.fori_loop(1, N, greet, 0)
    lax.fori_loop(1, Z, greet_z, 0)
    pl.semaphore_signal(barrier, inc=1, device_id=beside, device_id_type=MESH)

    k_in = pltpu.make_async_copy(k_ref, k_raw, raw_in.at[0])
    v_in = pltpu.make_async_copy(v_ref, v_raw, raw_in.at[1])
    q_in = pltpu.make_async_copy(q_ref, q_raw, raw_in.at[2])
    wp_in = pltpu.make_async_copy(wp_ref, wp, raw_in.at[3])
    k_in.start()
    v_in.start()
    q_in.start()
    wp_in.start()

    def ds(start, size):
        return pl.ds(pl.multiple_of(start, size), size)

    def own_tap(t):
        return pltpu.make_async_copy(
            taps_ref.at[t],
            w_all.at[t // 9, ds(z * CO, CO), ds(lax.rem(t, 9) * C, C)],
            w_own.at[t],
        )

    def tap_start(t, carry):
        own_tap(t).start()
        return carry

    lax.fori_loop(0, TAPS, tap_start, 0)
    square = (CO, CO)
    on = lax.broadcasted_iota(jnp.int32, square, 0) == lax.broadcasted_iota(jnp.int32, square, 1)
    bias = jnp.sum(
        jnp.where(on, jnp.broadcast_to(bias_ref[...], square), 0.0), axis=1, keepdims=True
    )
    high = bias.astype(BF).astype(F32)
    middle = (bias - high).astype(BF).astype(F32)
    low = bias - high - middle
    lane = lax.broadcasted_iota(jnp.int32, (CO, HD), 1)
    nought = jnp.zeros((CO, HD), F32)
    parts = jnp.where(lane == 0, high, jnp.where(lane == 1, middle, jnp.where(lane == 2, low, nought)))
    w_all[0, ds(z * CO, CO), PLANE:] = nought.astype(BF)
    w_all[1, ds(z * CO, CO), PLANE:] = nought.astype(BF)
    w_all[2, ds(z * CO, CO), PLANE:] = parts.astype(BF)
    v_t[HD:] = jnp.ones((EXTRA, LEN), BF)

    def by_head(copy, raw, out):
        copy.wait()

        def widen(b, carry):
            by_token[ds(b * TOK, TOK)] = raw[ds(b * TOK, TOK)].astype(F32)
            return carry

        lax.fori_loop(0, N, widen, 0)
        for h in range(N):
            out[h] = by_token[pl.ds(h, TOK, stride=N)].astype(BF)

    by_head(k_in, k_raw, k_out)
    pl.semaphore_wait(barrier, N + 2 * (Z - 1))

    def k_copy(t):
        to = lax.rem(me + t, N)
        return pltpu.make_async_remote_copy(
            src_ref=k_out.at[to], dst_ref=k_all.at[ds(me * TOK, TOK)],
            send_sem=k_send.at[t], recv_sem=k_recv.at[t],
            device_id={"seq": to}, device_id_type=MESH,
        )

    def v_copy(t):
        to = lax.rem(me + t, N)
        return pltpu.make_async_remote_copy(
            src_ref=v_out.at[to], dst_ref=v_all.at[ds(me * TOK, TOK)],
            send_sem=v_send.at[t], recv_sem=v_recv.at[t],
            device_id={"seq": to}, device_id_type=MESH,
        )

    def q_copy(t):
        to = lax.rem(me - t + N, N)
        return pltpu.make_async_remote_copy(
            src_ref=q_out.at[to], dst_ref=q_all.at[ds(t * TOK, TOK)],
            send_sem=q_send.at[t], recv_sem=q_recv.at[t],
            device_id={"seq": to}, device_id_type=MESH,
        )

    def o_copy(t):
        to = lax.rem(me + t, N)
        return pltpu.make_async_remote_copy(
            src_ref=o_buf.at[ds(t * TOK, TOK)], dst_ref=att.at[:, ds(me * HD, HD)],
            send_sem=o_send.at[t], recv_sem=o_recv.at[t],
            device_id={"seq": to}, device_id_type=MESH,
        )

    def every(act, copy, first=1, last=N):
        def body(t, carry):
            getattr(copy(t), act)()
            return carry
        lax.fori_loop(first, last, body, 0)

    pieces = [(-d, 1) for d in (1, 2, 3, 4)] + [(d, -1) for d in (1, 2, 3)]

    def shard_rows(d):
        return ds(lax.rem(z + d + Z, Z) * CO + half * HALF, HALF)

    def w_copy(i):
        d, turn = pieces[i]
        held = shard_rows(d + turn)
        return pltpu.make_async_remote_copy(
            src_ref=w_all.at[:, held], dst_ref=w_all.at[:, held],
            send_sem=w_send.at[i], recv_sem=w_recv.at[i],
            device_id={"rep": along_z(turn)}, device_id_type=MESH,
        )

    def core_copy(i):
        held = shard_rows(pieces[i][0])
        return pltpu.make_async_remote_copy(
            src_ref=w_all.at[:, held], dst_ref=w_all.at[:, held],
            send_sem=c_send.at[i], recv_sem=c_recv.at[i],
            device_id={"seq": other_core}, device_id_type=MESH,
        )

    def relay(i, *onward):
        w_copy(i).wait_recv()
        for j in onward:
            w_copy(j).start()
        core_copy(i).start()

    every("start", k_copy)
    every("wait", own_tap, 0, TAPS)
    w_copy(0).start()
    w_copy(4).start()
    by_head(v_in, v_raw, v_out)
    every("start", v_copy)
    by_head(q_in, q_raw, q_out)
    every("start", q_copy)

    def flip(place, block):
        v_t[:HD, place] = jnp.transpose(block)

    mine = ds(me * TOK, TOK)
    k_all[mine] = k_out[me]
    flip(mine, v_out[me])
    q_all[:TOK] = q_out[me]
    every("wait_recv", k_copy)

    factor = HD ** (-0.5) * math.log2(math.e)

    def query_block(u):
        q_t[...] = jnp.transpose(q_all[ds(u * BQ, BQ)])

    def scores(s_buf, keys, top):
        s = jnp.dot(k_all[keys], q_t[...], preferred_element_type=F32)
        s_buf[keys] = s
        return jnp.maximum(top, jnp.max(s.reshape(BK // 8, 8, BQ), axis=0))

    lowest = jnp.full((8, BQ), -jnp.inf, F32)

    def settle(top):
        m_buf[...] = jnp.broadcast_to(jnp.max(top, axis=0, keepdims=True), (8, BQ))

    def exps(s_buf, keys, m):
        below = s_buf[keys].reshape(BK // 8, 8, BQ) - m[None]
        return jnp.exp2(below * factor).reshape(BK, BQ).astype(BF)

    def weigh(p, keys):
        acc[...] += jnp.dot(v_t[:, keys], p, preferred_element_type=F32)

    def emit(u):
        o = (acc[:HD] / acc[HD : HD + 1]).astype(BF)
        o_buf[ds(u * BQ, BQ)] = jnp.transpose(o)

    def step(u, now, then):
        if then is not None:
            q_copy(2 * u + 2).wait_recv()
            q_copy(2 * u + 3).wait_recv()
            query_block(u + 1)
        m = m_buf[...]
        acc[...] = jnp.zeros_like(acc)

        def chunk(c, top):
            keys = ds(c * BK, BK)
            p = exps(now, keys, m)
            if then is not None:
                top = scores(then, keys, top)
            weigh(p, keys)
            return top

        top = lax.fori_loop(0, LEN // BK, chunk, lowest, unroll=2)
        if then is not None:
            settle(top)
        emit(u)

    q_copy(1).wait_recv()
    query_block(0)
    settle(
        lax.fori_loop(
            0, LEN // BK, lambda c, top: scores(s_even, ds(c * BK, BK), top), lowest
        )
    )
    relay(0, 1)
    relay(4, 5)

    def v_arrive(t, carry):
        v_copy(t).wait_recv()
        place = ds(lax.rem(me - t + N, N) * TOK, TOK)
        flip(place, v_all[place])
        return carry

    lax.fori_loop(1, N, v_arrive, 0)
    relay(1, 2)
    relay(5, 6)

    def steps(i, carry):
        step(2 * i, s_even, s_odd)

        @pl.when(i > 0)
        def _():
            o_copy(4 * i).start()

        o_copy(4 * i + 1).start()

        step(2 * i + 1, s_odd, s_even)
        o_copy(4 * i + 2).start()
        o_copy(4 * i + 3).start()

        @pl.when(i == 0)
        def _():
            relay(2, 3)
            relay(6)

        @pl.when(i == 2)
        def _():
            relay(3)

        return carry

    lax.fori_loop(0, STEPS // 2 - 1, steps, 0)
    step(STEPS - 2, s_even, s_odd)
    o_copy(N - 4).start()
    o_copy(N - 3).start()
    step(STEPS - 1, s_odd, None)
    o_copy(N - 2).start()
    o_copy(N - 1).start()
    own_o = pltpu.make_async_copy(o_buf.at[pl.ds(0, TOK)], att.at[:, ds(me * HD, HD)], o_recv.at[0])
    own_o.start()
    every("wait_send", k_copy)
    every("wait_send", v_copy)
    every("wait_send", q_copy)
    own_o.wait()
    every("wait_recv", o_copy)

    wp_in.wait()
    latent = jnp.dot(att[...], wp[...], preferred_element_type=F32).astype(BF)
    wide = latent.astype(F32)
    lat[0] = latent
    lat_copy = pltpu.make_async_remote_copy(
        src_ref=lat.at[0], dst_ref=lat.at[1], send_sem=b_send.at[0], recv_sem=b_recv.at[0],
        device_id=beside, device_id_type=MESH,
    )
    lat_copy.start()
    for f in range(FRAMES):
        first, last = f * TH * TW, (f + 1) * TH * TW - TW
        edges[pl.ds(f * TW, TW)] = wide[first : first + TW].astype(BF)
        edges[pl.ds((FRAMES + f) * TW, TW)] = wide[last : last + TW].astype(BF)
    for j in range(C // HD):
        lanes = pl.ds(j * HD, HD)
        by_lanes[j] = wide[:, j * HD : (j + 1) * HD]
        edges[pl.ds(64, 32), lanes] = by_lanes[j, pl.ds(0, FRAMES * TH, stride=TW)].astype(BF)
        edges[pl.ds(96, 32), lanes] = by_lanes[j, pl.ds(TW - 1, FRAMES * TH, stride=TW)].astype(BF)
        for n, start in enumerate((0, TW - 1, TW, 2 * TW - 1)):
            corner = by_lanes[j, pl.ds(start, 16, stride=2 * TW)]
            edges[pl.ds(CORNERS + 16 * n, 16), lanes] = corner.astype(BF)

    row, column = me // TILES, lax.rem(me, TILES)

    def rim_rows(n):
        return pl.ds(n * 32, 32) if n < 4 else pl.ds(CORNERS + (n - 4) * 16, 16)

    def rim_copy(n):
        at, size, down, right = RIMS[n]
        to = lax.rem(row + down + TILES, TILES) * TILES + lax.rem(column + right + TILES, TILES)
        return pltpu.make_async_remote_copy(
            src_ref=edges.at[pl.ds(at, size)], dst_ref=rims.at[0, rim_rows(n)],
            send_sem=e_send.at[n], recv_sem=e_recv.at[n],
            device_id={"seq": to}, device_id_type=MESH,
        )

    line = lax.broadcasted_iota(jnp.int32, (8, C), 0)
    stat[...] = jnp.where(
        line == 0,
        jnp.sum(wide, axis=0, keepdims=True),
        jnp.where(line == 1, jnp.sum(wide * wide, axis=0, keepdims=True), 0.0),
    )

    def stat_copy(t):
        return pltpu.make_async_remote_copy(
            src_ref=stat, dst_ref=stats.at[me],
            send_sem=t_send.at[t], recv_sem=t_recv.at[t],
            device_id={"seq": lax.rem(me + t, N)}, device_id_type=MESH,
        )

    every("start", stat_copy)
    for n in range(len(RIMS)):
        rim_copy(n).start()
    stats[me] = stat[...]
    ones[...] = jnp.where(
        lax.broadcasted_iota(jnp.int32, (128, TOK), 0) < 3, 1.0, 0.0
    ).astype(BF)
    gain, shift = gain_ref[...], shift_ref[...]
    every("wait_recv", stat_copy)

    size = C // GROUPS
    total = jnp.sum(stats[...], axis=0)
    lane = lax.broadcasted_iota(jnp.int32, (8, C), 1)
    for hop in (1, 2, 4, 8):
        after = pltpu.roll(total, C - hop, 1)
        before = pltpu.roll(total, hop, 1)
        total = total + jnp.where(lax.rem(lane // hop, 2) == 0, after, before)
    total = total / (LEN * size)
    mean = total[0:1]
    var = total[1:2] - mean * mean
    moments[0] = jnp.where(line == 0, mean, jnp.where(line == 1, lax.rsqrt(var + 1e-06), 0.0))

    def to_beside(n, ref):
        return pltpu.make_async_remote_copy(
            src_ref=ref.at[0], dst_ref=ref.at[1], send_sem=b_send.at[n], recv_sem=b_recv.at[n],
            device_id=beside, device_id_type=MESH,
        )

    moments_copy = to_beside(1, moments)
    rims_copy = to_beside(2, rims)
    moments_copy.start()
    for n in range(len(RIMS)):
        rim_copy(n).wait_recv()
    rims_copy.start()

    def decode(which, tile):
        mean, inverse = moments[which, 0:1], moments[which, 1:2]

        def activate(x):
            return jax.nn.silu((x.astype(F32) - mean) * inverse * gain + shift)

        inner = activate(lat[which])
        for f in range(FRAMES):
            for h in range(TH):
                field[f * (TH + 2) + 1 + h, pl.ds(8, TW)] = inner[
                    (f * TH + h) * TW : (f * TH + h + 1) * TW
                ]

        row, column = tile // TILES, lax.rem(tile, TILES)
        above, below = row > 0, row < TILES - 1
        before, after = column > 0, column < TILES - 1
        inside = (
            above, below, before, after,
            above & before, above & after, below & before, below & after,
        )
        for n in range(len(RIMS)):
            rim = jnp.where(inside[n], activate(rims[which, rim_rows(n)]), 0.0)
            for f in range(FRAMES):
                first = f * (TH + 2)
                last = first + TH + 1
                if n < 2:
                    field[last if n else first, pl.ds(8, TW)] = rim[f * TW : (f + 1) * TW]
                elif n < 4:
                    for h in range(TH):
                        k = f * TH + h
                        field[first + h + 1, pl.ds(7 if n == 2 else 16, 1)] = rim[k : k + 1]
                else:
                    k = 4 * f + (3 if n < 6 else 0)
                    side = 7 if n in (4, 6) else 16
                    field[first if n < 6 else last, pl.ds(side, 1)] = rim[k : k + 1]

        if which == 0:
            for i in range(len(pieces)):
                core_copy(i).wait_recv()
        by_frame[:2] = jnp.zeros((2, CH, TOK), F32)
        by_frame[2] = jnp.transpose(lat[which, :, ds(x_hi * CH, CH)]).astype(F32) + jnp.dot(
            w_all[2, :, PLANE:], ones[...], preferred_element_type=F32
        )

        def convolve(r, carry):
            x = jnp.concatenate(
                [
                    jnp.transpose(
                        jnp.concatenate(
                            [
                                field[r + (f * (TH + 2) + h), pl.ds(7 + s, TW)]
                                for f in range(FRAMES)
                                for h in range(TH)
                            ],
                            axis=0,
                        ).astype(BF)
                    )
                    for s in range(3)
                ],
                axis=0,
            )
            w = w_all[:, :, ds(r * 3 * C, 3 * C)].reshape(3 * CH, 3 * C)
            part = jnp.dot(w, x, preferred_element_type=F32)
            by_frame[...] += part.reshape(3, CH, TOK)
            return carry

        lax.fori_loop(0, 3, convolve, 0)
        at = lax.broadcasted_iota(jnp.int32, (CH, TOK), 1)
        frame = TH * TW
        one = jnp.where(at >= frame, pltpu.roll(by_frame[1], frame, 1), 0.0)
        two = jnp.where(at >= 2 * frame, pltpu.roll(by_frame[0], 2 * frame, 1), 0.0)
        out_t[which] = (by_frame[2] + one + two).astype(BF)

    def y_copy(t):
        theirs, hop = t // Z, lax.rem(t, Z)
        video = lax.rem(rep + theirs * Z, N)
        return pltpu.make_async_remote_copy(
            src_ref=out_t.at[theirs, ds(lax.rem(z + hop, Z) * CO, CO)], dst_ref=gathered.at[video],
            send_sem=y_send.at[t], recv_sem=y_recv.at[t],
            device_id={"seq": me + theirs * (twin - me), "rep": along_z(hop)},
            device_id_type=MESH,
        )

    decode(0, me)
    every("start", y_copy, 1, Z)
    gathered[rep] = out_t[0, ds(z * CO, CO)]
    lat_copy.wait_recv()
    moments_copy.wait_recv()
    rims_copy.wait_recv()
    decode(1, twin)
    every("start", y_copy, Z, N)
    for i in range(len(pieces)):
        w_copy(i).wait_send()
        core_copy(i).wait_send()
    for n in range(len(RIMS)):
        rim_copy(n).wait_send()
    lat_copy.wait_send()
    moments_copy.wait_send()
    rims_copy.wait_send()
    every("wait_send", o_copy)
    every("wait_send", stat_copy)
    every("wait_recv", y_copy)
    out_ref[...] = gathered[...]
    every("wait_send", y_copy)


def unit(q, k, v, taps, w_proj, gain, shift, bias):
    sem = pltpu.SemaphoreType.DMA
    vmem = pl.BlockSpec(memory_space=pltpu.VMEM)
    return pl.pallas_call(
        unit_kernel,
        out_shape=jax.ShapeDtypeStruct((N, CO, TOK), BF),
        in_specs=[pl.BlockSpec(memory_space=pl.ANY)] * 5 + [vmem] * 3,
        out_specs=vmem,
        scratch_shapes=[
            pltpu.VMEM((LEN, HD), BF),
            pltpu.VMEM((LEN, HD), BF),
            pltpu.VMEM((LEN, HD), BF),
            pltpu.VMEM((LEN, HD), F32),
            pltpu.VMEM((N, TOK, HD), BF),
            pltpu.VMEM((N, TOK, HD), BF),
            pltpu.VMEM((N, TOK, HD), BF),
            pltpu.VMEM((LEN, HD), BF),
            pltpu.VMEM((LEN, HD), BF),
            pltpu.VMEM((LEN, HD), BF),
            pltpu.VMEM((HD + EXTRA, LEN), BF),
            pltpu.VMEM((LEN, BQ), F32),
            pltpu.VMEM((LEN, BQ), F32),
            pltpu.VMEM((8, BQ), F32),
            pltpu.VMEM((HD, BQ), BF),
            pltpu.VMEM((HD + EXTRA, BQ), F32),
            pltpu.VMEM((LEN, HD), BF),
            pltpu.VMEM((TOK, N * HD), BF),
            pltpu.VMEM((N * HD, C), BF),
            pltpu.VMEM((3, CH, PLANE + 128), BF),
            pltpu.VMEM((2, TOK, C), BF),
            pltpu.VMEM((C // HD, TOK, HD), F32),
            pltpu.VMEM((RIM_ROWS, C), BF),
            pltpu.VMEM((2, RIM_ROWS, C), BF),
            pltpu.VMEM((8, C), F32),
            pltpu.VMEM((N, 8, C), F32),
            pltpu.VMEM((2, 8, C), F32),
            pltpu.VMEM((FRAMES * (TH + 2), PITCH, C), F32),
            pltpu.VMEM((128, TOK), BF),
            pltpu.VMEM((3, CH, TOK), F32),
            pltpu.VMEM((2, CH, TOK), BF),
            pltpu.VMEM((N, CO, TOK), BF),
        ]
        + [sem((N,))] * 8
        + [sem((4,)), sem((TAPS,))]
        + [sem((7,))] * 4
        + [sem((len(RIMS),))] * 2
        + [sem((N,))] * 2
        + [sem((3,))] * 2
        + [sem((N,))] * 2,
        compiler_params=pltpu.CompilerParams(
            collective_id=0, has_side_effects=True, vmem_limit_bytes=62 * 2**20
        ),
        cost_estimate=pl.CostEstimate(
            flops=4 * LEN * LEN * HD + 2 * TOK * TAPS * C * C,
            bytes_accessed=8 * 2**20,
            transcendentals=LEN * LEN,
        ),
        name="unit",
    )(q, k, v, taps, w_proj, gain, shift, bias)


def shards(queries, keys, values, w_proj, norm_gain, norm_bias, conv_weight, conv_bias):
    taps = conv_weight.reshape(TAPS, C, CO).transpose(0, 2, 1)
    q, k, v = (a.reshape(LEN, HD) for a in (queries, keys, values))
    out = unit(
        q, k, v, taps, w_proj, norm_gain[None], norm_bias[None], conv_bias[None]
    )
    return out.transpose(0, 2, 1).reshape(N, 1, FRAMES, TH, TW, CO)


def solution(mesh):
    return jax.shard_map(
        shards,
        mesh=mesh,
        in_specs=(
            P("rep", "seq", None, None),
            P("rep", "seq", None, None),
            P("rep", "seq", None, None),
            P(),
            P(),
            P(),
            P(None, None, None, None, "rep"),
            P("rep"),
        ),
        out_specs=P(None, "seq", None, None, None, "rep"),
        check_vma=False,
    )
```

```python
import math

import jax
import jax.numpy as jnp
from jax import lax
from jax.experimental import pallas as pl
from jax.experimental.pallas import tpu as pltpu
from jax.sharding import PartitionSpec as P

GROUPS = 32
FRAMES = 4
TH = 8
TW = 8
TILES = 4
HD = 128
N = 16
Z = 8
TOK = 256
LEN = N * TOK
C = 512
CO = C // N
HALF = CO // 2
TAPS = 27
PLANE = 9 * C
BQ = 512
BK = 256
ROUND = 4
EXTRA = 16
STEPS = LEN // BQ
PITCH = 24
BF = jnp.bfloat16
F32 = jnp.float32
MESH = pl.DeviceIdType.MESH
CORNERS = 4 * FRAMES * TW
RIMS = (
    (32, 32, 1, 0), (0, 32, -1, 0), (96, 32, 0, 1), (64, 32, 0, -1),
    (CORNERS + 48, 16, 1, 1), (CORNERS + 32, 16, 1, -1), (CORNERS + 16, 16, -1, 1), (CORNERS, 16, -1, -1),
)
RIM_ROWS = CORNERS + 4 * 16
CH = C // 2


def unit_kernel(
    q_ref, k_ref, v_ref, taps_ref, wp_ref, gain_ref, shift_ref, bias_ref, out_ref,
    q_raw, k_raw, v_raw, by_token, q_out, k_out, v_out,
    q_all, k_all, v_all, v_t, s_even, s_odd, m_buf, q_t, acc, o_buf, att, wp,
    w_all, lat, by_lanes, edges, rims, stat, stats, moments, field, ones, by_frame, out_t, gathered,
    q_send, q_recv, k_send, k_recv, v_send, v_recv, o_send, o_recv,
    raw_in, w_own, w_send, w_recv, c_send, c_recv, e_send, e_recv, t_send, t_recv, b_send, b_recv, y_send, y_recv,
):
    me = lax.axis_index("seq")
    rep = lax.axis_index("rep")
    x_hi = rep // Z
    z = lax.rem(rep, Z)
    half = lax.rem(me, 2)
    other_core = me + 1 - 2 * half
    twin = me + 2 - 4 * lax.rem(me // 2, 2)
    beside = {"seq": twin, "rep": lax.rem(rep + Z, N)}

    def along_z(d):
        return x_hi * Z + lax.rem(z + d + Z, Z)

    barrier = pltpu.get_barrier_semaphore()

    def greet(t, carry):
        pl.semaphore_signal(
            barrier, inc=1, device_id={"seq": lax.rem(me + t, N)}, device_id_type=MESH
        )
        return carry

    def greet_z(t, carry):
        for seq in (me, twin):
            pl.semaphore_signal(
                barrier, inc=1, device_id={"seq": seq, "rep": along_z(t)}, device_id_type=MESH
            )
        return carry

    lax.fori_loop(1, N, greet, 0)
    lax.fori_loop(1, Z, greet_z, 0)
    pl.semaphore_signal(barrier, inc=1, device_id=beside, device_id_type=MESH)

    k_in = pltpu.make_async_copy(k_ref, k_raw, raw_in.at[0])
    v_in = pltpu.make_async_copy(v_ref, v_raw, raw_in.at[1])
    q_in = pltpu.make_async_copy(q_ref, q_raw, raw_in.at[2])
    wp_in = pltpu.make_async_copy(wp_ref, wp, raw_in.at[3])
    k_in.start()
    v_in.start()
    q_in.start()
    wp_in.start()

    def ds(start, size):
        return pl.ds(pl.multiple_of(start, size), size)

    def own_tap(t):
        return pltpu.make_async_copy(
            taps_ref.at[t],
            w_all.at[t // 9, ds(z * CO, CO), ds(lax.rem(t, 9) * C, C)],
            w_own.at[t],
        )

    def tap_start(t, carry):
        own_tap(t).start()
        return carry

    lax.fori_loop(0, TAPS, tap_start, 0)
    square = (CO, CO)
    on = lax.broadcasted_iota(jnp.int32, square, 0) == lax.broadcasted_iota(jnp.int32, square, 1)
    bias = jnp.sum(
        jnp.where(on, jnp.broadcast_to(bias_ref[...], square), 0.0), axis=1, keepdims=True
    )
    high = bias.astype(BF).astype(F32)
    middle = (bias - high).astype(BF).astype(F32)
    low = bias - high - middle
    lane = lax.broadcasted_iota(jnp.int32, (CO, HD), 1)
    nought = jnp.zeros((CO, HD), F32)
    parts = jnp.where(lane == 0, high, jnp.where(lane == 1, middle, jnp.where(lane == 2, low, nought)))
    w_all[0, ds(z * CO, CO), PLANE:] = nought.astype(BF)
    w_all[1, ds(z * CO, CO), PLANE:] = nought.astype(BF)
    w_all[2, ds(z * CO, CO), PLANE:] = parts.astype(BF)
    v_t[HD:] = jnp.ones((EXTRA, LEN), BF)

    def widen(copy, raw):
        copy.wait()

        def body(b, carry):
            by_token[ds(b * TOK, TOK)] = raw[ds(b * TOK, TOK)].astype(F32)
            return carry

        lax.fori_loop(0, N, body, 0)

    def head(h):
        return by_token[pl.ds(h, TOK, stride=N)].astype(BF)

    def leave(out, copy, way):
        def body(t, carry):
            to = lax.rem(me + way * t + N, N)
            out[to] = head(to)
            copy(t).start()
            return carry

        lax.fori_loop(1, N, body, 0)

    def k_copy(t):
        to = lax.rem(me + t, N)
        return pltpu.make_async_remote_copy(
            src_ref=k_out.at[to], dst_ref=k_all.at[ds(me * TOK, TOK)],
            send_sem=k_send.at[t], recv_sem=k_recv.at[t],
            device_id={"seq": to}, device_id_type=MESH,
        )

    def v_copy(t):
        to = lax.rem(me + t, N)
        return pltpu.make_async_remote_copy(
            src_ref=v_out.at[to], dst_ref=v_all.at[ds(me * TOK, TOK)],
            send_sem=v_send.at[t], recv_sem=v_recv.at[t],
            device_id={"seq": to}, device_id_type=MESH,
        )

    def q_copy(t):
        to = lax.rem(me - t + N, N)
        return pltpu.make_async_remote_copy(
            src_ref=q_out.at[to], dst_ref=q_all.at[ds(t * TOK, TOK)],
            send_sem=q_send.at[t], recv_sem=q_recv.at[t],
            device_id={"seq": to}, device_id_type=MESH,
        )

    def o_copy(t):
        to = lax.rem(me + t, N)
        return pltpu.make_async_remote_copy(
            src_ref=o_buf.at[ds(t * TOK, TOK)], dst_ref=att.at[:, ds(me * HD, HD)],
            send_sem=o_send.at[t], recv_sem=o_recv.at[t],
            device_id={"seq": to}, device_id_type=MESH,
        )

    def every(act, copy, first=1, last=N):
        def body(t, carry):
            getattr(copy(t), act)()
            return carry
        lax.fori_loop(first, last, body, 0)

    pieces = [(-d, 1) for d in (1, 2, 3, 4)] + [(d, -1) for d in (1, 2, 3)]

    def shard_rows(d):
        return ds(lax.rem(z + d + Z, Z) * CO + half * HALF, HALF)

    def w_copy(i):
        d, turn = pieces[i]
        held = shard_rows(d + turn)
        return pltpu.make_async_remote_copy(
            src_ref=w_all.at[:, held], dst_ref=w_all.at[:, held],
            send_sem=w_send.at[i], recv_sem=w_recv.at[i],
            device_id={"rep": along_z(turn)}, device_id_type=MESH,
        )

    def core_copy(i):
        held = shard_rows(pieces[i][0])
        return pltpu.make_async_remote_copy(
            src_ref=w_all.at[:, held], dst_ref=w_all.at[:, held],
            send_sem=c_send.at[i], recv_sem=c_recv.at[i],
            device_id={"seq": other_core}, device_id_type=MESH,
        )

    def relay(i, *onward):
        w_copy(i).wait_recv()
        for j in onward:
            w_copy(j).start()
        core_copy(i).start()

    def flip(place, block):
        v_t[:HD, place] = jnp.transpose(block)

    mine = ds(me * TOK, TOK)
    widen(k_in, k_raw)
    pl.semaphore_wait(barrier, N + 2 * (Z - 1))
    leave(k_out, k_copy, 1)
    k_all[mine] = head(me)
    every("wait", own_tap, 0, TAPS)
    w_copy(0).start()
    w_copy(4).start()
    widen(v_in, v_raw)
    leave(v_out, v_copy, 1)
    flip(mine, head(me))
    widen(q_in, q_raw)
    leave(q_out, q_copy, -1)
    q_all[:TOK] = head(me)

    every("wait_recv", k_copy)

    factor = HD ** (-0.5) * math.log2(math.e)

    def query_block(u):
        q_t[...] = jnp.transpose(q_all[ds(u * BQ, BQ)])

    def scores(s_buf, keys, top):
        s = jnp.dot(k_all[keys], q_t[...], preferred_element_type=F32)
        s_buf[keys] = s
        return jnp.maximum(top, jnp.max(s.reshape(BK // 8, 8, BQ), axis=0))

    lowest = jnp.full((8, BQ), -jnp.inf, F32)

    def settle(top):
        m_buf[...] = jnp.broadcast_to(jnp.max(top, axis=0, keepdims=True), (8, BQ))

    def exps(s_buf, keys, m):
        below = s_buf[keys].reshape(BK // 8, 8, BQ) - m[None]
        return jnp.exp2(below * factor).reshape(BK, BQ).astype(BF)

    def weigh(p, keys):
        return jnp.dot(v_t[:, keys], p, preferred_element_type=F32)

    def emit(u):
        o = (acc[:HD] / acc[HD : HD + 1]).astype(BF)
        o_buf[ds(u * BQ, BQ)] = jnp.transpose(o)

    def step(u, now, then):
        if then is not None:
            q_copy(2 * u + 2).wait_recv()
            q_copy(2 * u + 3).wait_recv()
            query_block(u + 1)
        m = m_buf[...]
        acc[...] = jnp.zeros_like(acc)

        def chunks(c, top):
            total = None
            for i in range(ROUND):
                keys = ds((c * ROUND + i) * BK, BK)
                p = exps(now, keys, m)
                if then is not None:
                    top = scores(then, keys, top)
                got = weigh(p, keys)
                total = got if total is None else total + got
            acc[...] += total
            return top

        top = lax.fori_loop(0, LEN // (ROUND * BK), chunks, lowest)
        if then is not None:
            settle(top)
        emit(u)

    q_copy(1).wait_recv()
    query_block(0)
    settle(
        lax.fori_loop(
            0, LEN // BK, lambda c, top: scores(s_even, ds(c * BK, BK), top), lowest, unroll=ROUND
        )
    )
    relay(0, 1)
    relay(4, 5)

    def v_arrive(t, carry):
        v_copy(t).wait_recv()
        place = ds(lax.rem(me - t + N, N) * TOK, TOK)
        flip(place, v_all[place])
        return carry

    lax.fori_loop(1, N, v_arrive, 0)
    relay(1, 2)
    relay(5, 6)

    def steps(i, carry):
        step(2 * i, s_even, s_odd)

        @pl.when(i > 0)
        def _():
            o_copy(4 * i).start()

        o_copy(4 * i + 1).start()

        step(2 * i + 1, s_odd, s_even)
        o_copy(4 * i + 2).start()
        o_copy(4 * i + 3).start()

        @pl.when(i == 0)
        def _():
            relay(2, 3)
            relay(6)

        @pl.when(i == 2)
        def _():
            relay(3)

        return carry

    lax.fori_loop(0, STEPS // 2 - 1, steps, 0)
    step(STEPS - 2, s_even, s_odd)
    o_copy(N - 4).start()
    o_copy(N - 3).start()
    step(STEPS - 1, s_odd, None)
    o_copy(N - 2).start()
    o_copy(N - 1).start()
    own_o = pltpu.make_async_copy(o_buf.at[pl.ds(0, TOK)], att.at[:, ds(me * HD, HD)], o_recv.at[0])
    own_o.start()
    own_o.wait()
    every("wait_recv", o_copy)

    wp_in.wait()
    latent = jnp.dot(att[...], wp[...], preferred_element_type=F32).astype(BF)
    wide = latent.astype(F32)
    line = lax.broadcasted_iota(jnp.int32, (8, C), 0)
    stat[...] = jnp.where(
        line == 0,
        jnp.sum(wide, axis=0, keepdims=True),
        jnp.where(line == 1, jnp.sum(wide * wide, axis=0, keepdims=True), 0.0),
    )

    def stat_copy(t):
        return pltpu.make_async_remote_copy(
            src_ref=stat, dst_ref=stats.at[me],
            send_sem=t_send.at[t], recv_sem=t_recv.at[t],
            device_id={"seq": lax.rem(me + t, N)}, device_id_type=MESH,
        )

    every("start", stat_copy)
    lat[0] = latent
    lat_copy = pltpu.make_async_remote_copy(
        src_ref=lat.at[0], dst_ref=lat.at[1], send_sem=b_send.at[0], recv_sem=b_recv.at[0],
        device_id=beside, device_id_type=MESH,
    )
    lat_copy.start()
    for f in range(FRAMES):
        first, last = f * TH * TW, (f + 1) * TH * TW - TW
        edges[pl.ds(f * TW, TW)] = wide[first : first + TW].astype(BF)
        edges[pl.ds((FRAMES + f) * TW, TW)] = wide[last : last + TW].astype(BF)
    for j in range(C // HD):
        lanes = pl.ds(j * HD, HD)
        by_lanes[j] = wide[:, j * HD : (j + 1) * HD]
        edges[pl.ds(64, 32), lanes] = by_lanes[j, pl.ds(0, FRAMES * TH, stride=TW)].astype(BF)
        edges[pl.ds(96, 32), lanes] = by_lanes[j, pl.ds(TW - 1, FRAMES * TH, stride=TW)].astype(BF)
        for n, start in enumerate((0, TW - 1, TW, 2 * TW - 1)):
            corner = by_lanes[j, pl.ds(start, 16, stride=2 * TW)]
            edges[pl.ds(CORNERS + 16 * n, 16), lanes] = corner.astype(BF)

    row, column = me // TILES, lax.rem(me, TILES)

    def rim_rows(n):
        return pl.ds(n * 32, 32) if n < 4 else pl.ds(CORNERS + (n - 4) * 16, 16)

    def rim_copy(n):
        at, size, down, right = RIMS[n]
        to = lax.rem(row + down + TILES, TILES) * TILES + lax.rem(column + right + TILES, TILES)
        return pltpu.make_async_remote_copy(
            src_ref=edges.at[pl.ds(at, size)], dst_ref=rims.at[0, rim_rows(n)],
            send_sem=e_send.at[n], recv_sem=e_recv.at[n],
            device_id={"seq": to}, device_id_type=MESH,
        )

    for n in range(len(RIMS)):
        rim_copy(n).start()
    stats[me] = stat[...]
    ones[...] = jnp.where(
        lax.broadcasted_iota(jnp.int32, (128, TOK), 0) < 3, 1.0, 0.0
    ).astype(BF)
    for i in range(len(pieces)):
        core_copy(i).wait_recv()

    def residual(which):
        by_frame[:2] = jnp.zeros((2, CH, TOK), F32)
        bias = jnp.dot(w_all[2, :, PLANE:], ones[...], preferred_element_type=F32)
        by_frame[2] = jnp.transpose(lat[which, :, ds(x_hi * CH, CH)]).astype(F32) + bias

    residual(0)
    gain, shift = gain_ref[...], shift_ref[...]
    every("wait_recv", stat_copy)

    size = C // GROUPS
    total = jnp.sum(stats[...], axis=0)
    lane = lax.broadcasted_iota(jnp.int32, (8, C), 1)
    for hop in (1, 2, 4, 8):
        after = pltpu.roll(total, C - hop, 1)
        before = pltpu.roll(total, hop, 1)
        total = total + jnp.where(lax.rem(lane // hop, 2) == 0, after, before)
    total = total / (LEN * size)
    mean = total[0:1]
    var = total[1:2] - mean * mean
    moments[0] = jnp.where(line == 0, mean, jnp.where(line == 1, lax.rsqrt(var + 1e-06), 0.0))

    def to_beside(n, ref):
        return pltpu.make_async_remote_copy(
            src_ref=ref.at[0], dst_ref=ref.at[1], send_sem=b_send.at[n], recv_sem=b_recv.at[n],
            device_id=beside, device_id_type=MESH,
        )

    moments_copy = to_beside(1, moments)
    rims_copy = to_beside(2, rims)
    moments_copy.start()
    for n in range(len(RIMS)):
        rim_copy(n).wait_recv()
    rims_copy.start()

    def decode(which, tile):
        mean, inverse = moments[which, 0:1], moments[which, 1:2]

        def activate(x):
            return jax.nn.silu((x.astype(F32) - mean) * inverse * gain + shift)

        inner = activate(lat[which])
        for f in range(FRAMES):
            for h in range(TH):
                field[f * (TH + 2) + 1 + h, pl.ds(8, TW)] = inner[
                    (f * TH + h) * TW : (f * TH + h + 1) * TW
                ]

        row, column = tile // TILES, lax.rem(tile, TILES)
        above, below = row > 0, row < TILES - 1
        before, after = column > 0, column < TILES - 1
        inside = (
            above, below, before, after,
            above & before, above & after, below & before, below & after,
        )
        for n in range(len(RIMS)):
            rim = jnp.where(inside[n], activate(rims[which, rim_rows(n)]), 0.0)
            for f in range(FRAMES):
                first = f * (TH + 2)
                last = first + TH + 1
                if n < 2:
                    field[last if n else first, pl.ds(8, TW)] = rim[f * TW : (f + 1) * TW]
                elif n < 4:
                    for h in range(TH):
                        k = f * TH + h
                        field[first + h + 1, pl.ds(7 if n == 2 else 16, 1)] = rim[k : k + 1]
                else:
                    k = 4 * f + (3 if n < 6 else 0)
                    side = 7 if n in (4, 6) else 16
                    field[first if n < 6 else last, pl.ds(side, 1)] = rim[k : k + 1]

        if which:
            residual(which)

        def convolve(r, carry):
            x = jnp.concatenate(
                [
                    jnp.transpose(
                        jnp.concatenate(
                            [
                                field[r + (f * (TH + 2) + h), pl.ds(7 + s, TW)]
                                for f in range(FRAMES)
                                for h in range(TH)
                            ],
                            axis=0,
                        ).astype(BF)
                    )
                    for s in range(3)
                ],
                axis=0,
            )
            w = w_all[:, :, ds(r * 3 * C, 3 * C)].reshape(3 * CH, 3 * C)
            part = jnp.dot(w, x, preferred_element_type=F32)
            by_frame[...] += part.reshape(3, CH, TOK)
            return carry

        lax.fori_loop(0, 3, convolve, 0)
        at = lax.broadcasted_iota(jnp.int32, (CH, TOK), 1)
        frame = TH * TW
        one = jnp.where(at >= frame, pltpu.roll(by_frame[1], frame, 1), 0.0)
        two = jnp.where(at >= 2 * frame, pltpu.roll(by_frame[0], 2 * frame, 1), 0.0)
        out_t[which] = (by_frame[2] + one + two).astype(BF)

    def y_copy(t):
        theirs, hop = t // Z, lax.rem(t, Z)
        video = lax.rem(rep + theirs * Z, N)
        return pltpu.make_async_remote_copy(
            src_ref=out_t.at[theirs, ds(lax.rem(z + hop, Z) * CO, CO)], dst_ref=gathered.at[video],
            send_sem=y_send.at[t], recv_sem=y_recv.at[t],
            device_id={"seq": me + theirs * (twin - me), "rep": along_z(hop)},
            device_id_type=MESH,
        )

    decode(0, me)
    every("start", y_copy, 1, Z)
    gathered[rep] = out_t[0, ds(z * CO, CO)]
    lat_copy.wait_recv()
    moments_copy.wait_recv()
    rims_copy.wait_recv()
    decode(1, twin)
    every("start", y_copy, Z, N)
    for i in range(len(pieces)):
        w_copy(i).wait_send()
        core_copy(i).wait_send()
    for n in range(len(RIMS)):
        rim_copy(n).wait_send()
    lat_copy.wait_send()
    moments_copy.wait_send()
    rims_copy.wait_send()
    every("wait_send", k_copy)
    every("wait_send", v_copy)
    every("wait_send", q_copy)
    every("wait_send", o_copy)
    every("wait_send", stat_copy)
    every("wait_recv", y_copy)
    out_ref[...] = gathered[...]
    every("wait_send", y_copy)


def unit(q, k, v, taps, w_proj, gain, shift, bias):
    sem = pltpu.SemaphoreType.DMA
    vmem = pl.BlockSpec(memory_space=pltpu.VMEM)
    return pl.pallas_call(
        unit_kernel,
        out_shape=jax.ShapeDtypeStruct((N, CO, TOK), BF),
        in_specs=[pl.BlockSpec(memory_space=pl.ANY)] * 5 + [vmem] * 3,
        out_specs=vmem,
        scratch_shapes=[
            pltpu.VMEM((LEN, HD), BF),
            pltpu.VMEM((LEN, HD), BF),
            pltpu.VMEM((LEN, HD), BF),
            pltpu.VMEM((LEN, HD), F32),
            pltpu.VMEM((N, TOK, HD), BF),
            pltpu.VMEM((N, TOK, HD), BF),
            pltpu.VMEM((N, TOK, HD), BF),
            pltpu.VMEM((LEN, HD), BF),
            pltpu.VMEM((LEN, HD), BF),
            pltpu.VMEM((LEN, HD), BF),
            pltpu.VMEM((HD + EXTRA, LEN), BF),
            pltpu.VMEM((LEN, BQ), F32),
            pltpu.VMEM((LEN, BQ), F32),
            pltpu.VMEM((8, BQ), F32),
            pltpu.VMEM((HD, BQ), BF),
            pltpu.VMEM((HD + EXTRA, BQ), F32),
            pltpu.VMEM((LEN, HD), BF),
            pltpu.VMEM((TOK, N * HD), BF),
            pltpu.VMEM((N * HD, C), BF),
            pltpu.VMEM((3, CH, PLANE + 128), BF),
            pltpu.VMEM((2, TOK, C), BF),
            pltpu.VMEM((C // HD, TOK, HD), F32),
            pltpu.VMEM((RIM_ROWS, C), BF),
            pltpu.VMEM((2, RIM_ROWS, C), BF),
            pltpu.VMEM((8, C), F32),
            pltpu.VMEM((N, 8, C), F32),
            pltpu.VMEM((2, 8, C), F32),
            pltpu.VMEM((FRAMES * (TH + 2), PITCH, C), F32),
            pltpu.VMEM((128, TOK), BF),
            pltpu.VMEM((3, CH, TOK), F32),
            pltpu.VMEM((2, CH, TOK), BF),
            pltpu.VMEM((N, CO, TOK), BF),
        ]
        + [sem((N,))] * 8
        + [sem((4,)), sem((TAPS,))]
        + [sem((7,))] * 4
        + [sem((len(RIMS),))] * 2
        + [sem((N,))] * 2
        + [sem((3,))] * 2
        + [sem((N,))] * 2,
        compiler_params=pltpu.CompilerParams(
            collective_id=0, has_side_effects=True, vmem_limit_bytes=62 * 2**20
        ),
        cost_estimate=pl.CostEstimate(
            flops=4 * LEN * LEN * HD + 2 * TOK * TAPS * C * C,
            bytes_accessed=8 * 2**20,
            transcendentals=LEN * LEN,
        ),
        name="unit",
    )(q, k, v, taps, w_proj, gain, shift, bias)


def shards(queries, keys, values, w_proj, norm_gain, norm_bias, conv_weight, conv_bias):
    taps = conv_weight.reshape(TAPS, C, CO).transpose(0, 2, 1)
    q, k, v = (a.reshape(LEN, HD) for a in (queries, keys, values))
    out = unit(
        q, k, v, taps, w_proj, norm_gain[None], norm_bias[None], conv_bias[None]
    )
    return out.transpose(0, 2, 1).reshape(N, 1, FRAMES, TH, TW, CO)


def solution(mesh):
    return jax.shard_map(
        shards,
        mesh=mesh,
        in_specs=(
            P("rep", "seq", None, None),
            P("rep", "seq", None, None),
            P("rep", "seq", None, None),
            P(),
            P(),
            P(),
            P(None, None, None, None, "rep"),
            P("rep"),
        ),
        out_specs=P(None, "seq", None, None, None, "rep"),
        check_vma=False,
    )
```

```python
import math

import jax
import jax.numpy as jnp
from jax import lax
from jax.experimental import pallas as pl
from jax.experimental.pallas import tpu as pltpu
from jax.sharding import PartitionSpec as P

GROUPS = 32
FRAMES = 4
TH = 8
TW = 8
TILES = 4
HD = 128
N = 16
Z = 8
TOK = 256
LEN = N * TOK
C = 512
CO = C // N
HALF = CO // 2
TAPS = 27
PLANE = 9 * C
BQ = 512
BK = 256
ROUND = 4
EXTRA = 16
STEPS = LEN // BQ
PITCH = 24
BF = jnp.bfloat16
F32 = jnp.float32
MESH = pl.DeviceIdType.MESH
CORNERS = 4 * FRAMES * TW
RIMS = (
    (32, 32, 1, 0), (0, 32, -1, 0), (96, 32, 0, 1), (64, 32, 0, -1),
    (CORNERS + 48, 16, 1, 1), (CORNERS + 32, 16, 1, -1), (CORNERS + 16, 16, -1, 1), (CORNERS, 16, -1, -1),
)
RIM_ROWS = CORNERS + 4 * 16
CH = C // 2


def unit_kernel(
    q_ref, k_ref, v_ref, taps_ref, wp_ref, gain_ref, shift_ref, bias_ref, out_ref,
    q_raw, k_raw, v_raw, by_token, q_out, k_out, v_out,
    q_all, k_all, v_all, v_t, s_even, s_odd, m_buf, q_t, acc, o_buf, att, wp,
    w_all, lat, by_lanes, edges, rims, stat, stats, moments, field, ones, by_frame, out_t, gathered,
    q_send, q_recv, k_send, k_recv, v_send, v_recv, o_send, o_recv,
    raw_in, w_own, w_send, w_recv, c_send, c_recv, e_send, e_recv, t_send, t_recv, b_send, b_recv, y_send, y_recv,
):
    me = lax.axis_index("seq")
    rep = lax.axis_index("rep")
    x_hi = rep // Z
    z = lax.rem(rep, Z)
    half = lax.rem(me, 2)
    other_core = me + 1 - 2 * half
    twin = me + 2 - 4 * lax.rem(me // 2, 2)
    beside = {"seq": twin, "rep": lax.rem(rep + Z, N)}

    def along_z(d):
        return x_hi * Z + lax.rem(z + d + Z, Z)

    barrier = pltpu.get_barrier_semaphore()

    def greet(t, carry):
        pl.semaphore_signal(
            barrier, inc=1, device_id={"seq": lax.rem(me + t, N)}, device_id_type=MESH
        )
        return carry

    def greet_z(t, carry):
        for seq in (me, twin):
            pl.semaphore_signal(
                barrier, inc=1, device_id={"seq": seq, "rep": along_z(t)}, device_id_type=MESH
            )
        return carry

    lax.fori_loop(1, N, greet, 0)
    lax.fori_loop(1, Z, greet_z, 0)
    pl.semaphore_signal(barrier, inc=1, device_id=beside, device_id_type=MESH)

    k_in = pltpu.make_async_copy(k_ref, k_raw, raw_in.at[0])
    v_in = pltpu.make_async_copy(v_ref, v_raw, raw_in.at[1])
    q_in = pltpu.make_async_copy(q_ref, q_raw, raw_in.at[2])
    wp_in = pltpu.make_async_copy(wp_ref, wp, raw_in.at[3])
    k_in.start()
    v_in.start()
    q_in.start()
    wp_in.start()

    def ds(start, size):
        return pl.ds(pl.multiple_of(start, size), size)

    def own_tap(t):
        return pltpu.make_async_copy(
            taps_ref.at[t],
            w_all.at[t // 9, ds(z * CO, CO), ds(lax.rem(t, 9) * C, C)],
            w_own.at[t],
        )

    def tap_start(t, carry):
        own_tap(t).start()
        return carry

    lax.fori_loop(0, TAPS, tap_start, 0)
    square = (CO, CO)
    on = lax.broadcasted_iota(jnp.int32, square, 0) == lax.broadcasted_iota(jnp.int32, square, 1)
    bias = jnp.sum(
        jnp.where(on, jnp.broadcast_to(bias_ref[...], square), 0.0), axis=1, keepdims=True
    )
    high = bias.astype(BF).astype(F32)
    middle = (bias - high).astype(BF).astype(F32)
    low = bias - high - middle
    lane = lax.broadcasted_iota(jnp.int32, (CO, HD), 1)
    nought = jnp.zeros((CO, HD), F32)
    parts = jnp.where(lane == 0, high, jnp.where(lane == 1, middle, jnp.where(lane == 2, low, nought)))
    w_all[0, ds(z * CO, CO), PLANE:] = nought.astype(BF)
    w_all[1, ds(z * CO, CO), PLANE:] = nought.astype(BF)
    w_all[2, ds(z * CO, CO), PLANE:] = parts.astype(BF)
    v_t[HD:] = jnp.ones((EXTRA, LEN), BF)

    def widen(copy, raw):
        copy.wait()

        def body(b, carry):
            by_token[ds(b * TOK, TOK)] = raw[ds(b * TOK, TOK)].astype(F32)
            return carry

        lax.fori_loop(0, N, body, 0)

    def head(h):
        return by_token[pl.ds(h, TOK, stride=N)].astype(BF)

    def leave(out, copy, way, first=1, last=N):
        def body(t, carry):
            to = lax.rem(me + way * t + N, N)
            out[to] = head(to)
            copy(t).start()
            return carry

        lax.fori_loop(first, last, body, 0)

    def k_copy(t):
        to = lax.rem(me + t, N)
        return pltpu.make_async_remote_copy(
            src_ref=k_out.at[to], dst_ref=k_all.at[ds(me * TOK, TOK)],
            send_sem=k_send.at[t], recv_sem=k_recv.at[t],
            device_id={"seq": to}, device_id_type=MESH,
        )

    def v_copy(t):
        to = lax.rem(me + t, N)
        return pltpu.make_async_remote_copy(
            src_ref=v_out.at[to], dst_ref=v_all.at[ds(me * TOK, TOK)],
            send_sem=v_send.at[t], recv_sem=v_recv.at[t],
            device_id={"seq": to}, device_id_type=MESH,
        )

    def q_copy(t):
        to = lax.rem(me - t + N, N)
        return pltpu.make_async_remote_copy(
            src_ref=q_out.at[to], dst_ref=q_all.at[ds(t * TOK, TOK)],
            send_sem=q_send.at[t], recv_sem=q_recv.at[t],
            device_id={"seq": to}, device_id_type=MESH,
        )

    def o_copy(t):
        to = lax.rem(me + t, N)
        return pltpu.make_async_remote_copy(
            src_ref=o_buf.at[ds(t * TOK, TOK)], dst_ref=att.at[:, ds(me * HD, HD)],
            send_sem=o_send.at[t], recv_sem=o_recv.at[t],
            device_id={"seq": to}, device_id_type=MESH,
        )

    def every(act, copy, first=1, last=N):
        def body(t, carry):
            getattr(copy(t), act)()
            return carry
        lax.fori_loop(first, last, body, 0)

    pieces = [(-d, 1) for d in (1, 2, 3, 4)] + [(d, -1) for d in (1, 2, 3)]

    def shard_rows(d):
        return ds(lax.rem(z + d + Z, Z) * CO + half * HALF, HALF)

    def w_copy(i):
        d, turn = pieces[i]
        held = shard_rows(d + turn)
        return pltpu.make_async_remote_copy(
            src_ref=w_all.at[:, held], dst_ref=w_all.at[:, held],
            send_sem=w_send.at[i], recv_sem=w_recv.at[i],
            device_id={"rep": along_z(turn)}, device_id_type=MESH,
        )

    def core_copy(i):
        held = shard_rows(pieces[i][0])
        return pltpu.make_async_remote_copy(
            src_ref=w_all.at[:, held], dst_ref=w_all.at[:, held],
            send_sem=c_send.at[i], recv_sem=c_recv.at[i],
            device_id={"seq": other_core}, device_id_type=MESH,
        )

    def relay(i, *onward):
        w_copy(i).wait_recv()
        for j in onward:
            w_copy(j).start()
        core_copy(i).start()

    def flip(place, block):
        v_t[:HD, place] = jnp.transpose(block)

    mine = ds(me * TOK, TOK)
    widen(k_in, k_raw)
    pl.semaphore_wait(barrier, N + 2 * (Z - 1))
    leave(k_out, k_copy, 1)
    k_all[mine] = head(me)
    widen(v_in, v_raw)
    leave(v_out, v_copy, 1)
    flip(mine, head(me))
    widen(q_in, q_raw)
    leave(q_out, q_copy, -1, 1, 8)
    every("wait", own_tap, 0, TAPS)
    w_copy(0).start()
    w_copy(4).start()
    leave(q_out, q_copy, -1, 8, N)
    q_all[:TOK] = head(me)

    every("wait_recv", k_copy)

    factor = HD ** (-0.5) * math.log2(math.e)

    def query_block(u):
        q_t[...] = jnp.transpose(q_all[ds(u * BQ, BQ)])

    def scores(s_buf, keys, top):
        s = jnp.dot(k_all[keys], q_t[...], preferred_element_type=F32)
        s_buf[keys] = s
        return jnp.maximum(top, jnp.max(s.reshape(BK // 8, 8, BQ), axis=0))

    lowest = jnp.full((8, BQ), -jnp.inf, F32)

    def settle(top):
        m_buf[...] = jnp.broadcast_to(jnp.max(top, axis=0, keepdims=True), (8, BQ))

    def exps(s_buf, keys, m):
        below = s_buf[keys].reshape(BK // 8, 8, BQ) - m[None]
        return jnp.exp2(below * factor).reshape(BK, BQ).astype(BF)

    def weigh(p, keys):
        return jnp.dot(v_t[:, keys], p, preferred_element_type=F32)

    def emit(u):
        o = (acc[:HD] / acc[HD : HD + 1]).astype(BF)
        o_buf[ds(u * BQ, BQ)] = jnp.transpose(o)

    def step(u, now, then):
        if then is not None:
            q_copy(2 * u + 2).wait_recv()
            q_copy(2 * u + 3).wait_recv()
            query_block(u + 1)
        m = m_buf[...]
        acc[...] = jnp.zeros_like(acc)

        def chunks(c, top):
            total = None
            for i in range(ROUND):
                keys = ds((c * ROUND + i) * BK, BK)
                p = exps(now, keys, m)
                if then is not None:
                    top = scores(then, keys, top)
                got = weigh(p, keys)
                total = got if total is None else total + got
            acc[...] += total
            return top

        top = lax.fori_loop(0, LEN // (ROUND * BK), chunks, lowest)
        if then is not None:
            settle(top)
        emit(u)

    q_copy(1).wait_recv()
    query_block(0)
    settle(
        lax.fori_loop(
            0, LEN // BK, lambda c, top: scores(s_even, ds(c * BK, BK), top), lowest, unroll=ROUND
        )
    )

    def v_arrive(t, carry):
        v_copy(t).wait_recv()
        place = ds(lax.rem(me - t + N, N) * TOK, TOK)
        flip(place, v_all[place])
        return carry

    lax.fori_loop(1, N, v_arrive, 0)

    def steps(i, carry):
        step(2 * i, s_even, s_odd)

        @pl.when(i > 0)
        def _():
            o_copy(4 * i).start()

        o_copy(4 * i + 1).start()

        @pl.when(i == 1)
        def _():
            relay(0, 1)
            relay(4, 5)

        @pl.when(i == 2)
        def _():
            relay(1, 2)
            relay(5, 6)

        step(2 * i + 1, s_odd, s_even)
        o_copy(4 * i + 2).start()
        o_copy(4 * i + 3).start()
        return carry

    lax.fori_loop(0, STEPS // 2 - 1, steps, 0)
    step(STEPS - 2, s_even, s_odd)
    o_copy(N - 4).start()
    o_copy(N - 3).start()
    relay(2, 3)
    relay(6)
    step(STEPS - 1, s_odd, None)
    o_copy(N - 2).start()
    o_copy(N - 1).start()
    own_o = pltpu.make_async_copy(o_buf.at[pl.ds(0, TOK)], att.at[:, ds(me * HD, HD)], o_recv.at[0])
    own_o.start()
    own_o.wait()
    every("wait_recv", o_copy)

    wp_in.wait()
    latent = jnp.dot(att[...], wp[...], preferred_element_type=F32).astype(BF)
    wide = latent.astype(F32)
    line = lax.broadcasted_iota(jnp.int32, (8, C), 0)
    stat[...] = jnp.where(
        line == 0,
        jnp.sum(wide, axis=0, keepdims=True),
        jnp.where(line == 1, jnp.sum(wide * wide, axis=0, keepdims=True), 0.0),
    )

    def stat_copy(t):
        return pltpu.make_async_remote_copy(
            src_ref=stat, dst_ref=stats.at[me],
            send_sem=t_send.at[t], recv_sem=t_recv.at[t],
            device_id={"seq": lax.rem(me + t, N)}, device_id_type=MESH,
        )

    every("start", stat_copy)
    lat[0] = latent
    lat_copy = pltpu.make_async_remote_copy(
        src_ref=lat.at[0], dst_ref=lat.at[1], send_sem=b_send.at[0], recv_sem=b_recv.at[0],
        device_id=beside, device_id_type=MESH,
    )
    lat_copy.start()
    for f in range(FRAMES):
        first, last = f * TH * TW, (f + 1) * TH * TW - TW
        edges[pl.ds(f * TW, TW)] = wide[first : first + TW].astype(BF)
        edges[pl.ds((FRAMES + f) * TW, TW)] = wide[last : last + TW].astype(BF)
    for j in range(C // HD):
        lanes = pl.ds(j * HD, HD)
        by_lanes[j] = wide[:, j * HD : (j + 1) * HD]
        edges[pl.ds(64, 32), lanes] = by_lanes[j, pl.ds(0, FRAMES * TH, stride=TW)].astype(BF)
        edges[pl.ds(96, 32), lanes] = by_lanes[j, pl.ds(TW - 1, FRAMES * TH, stride=TW)].astype(BF)
        for n, start in enumerate((0, TW - 1, TW, 2 * TW - 1)):
            corner = by_lanes[j, pl.ds(start, 16, stride=2 * TW)]
            edges[pl.ds(CORNERS + 16 * n, 16), lanes] = corner.astype(BF)

    row, column = me // TILES, lax.rem(me, TILES)

    def rim_rows(n):
        return pl.ds(n * 32, 32) if n < 4 else pl.ds(CORNERS + (n - 4) * 16, 16)

    def rim_copy(n):
        at, size, down, right = RIMS[n]
        to = lax.rem(row + down + TILES, TILES) * TILES + lax.rem(column + right + TILES, TILES)
        return pltpu.make_async_remote_copy(
            src_ref=edges.at[pl.ds(at, size)], dst_ref=rims.at[0, rim_rows(n)],
            send_sem=e_send.at[n], recv_sem=e_recv.at[n],
            device_id={"seq": to}, device_id_type=MESH,
        )

    for n in range(len(RIMS)):
        rim_copy(n).start()
    stats[me] = stat[...]
    ones[...] = jnp.where(
        lax.broadcasted_iota(jnp.int32, (128, TOK), 0) < 3, 1.0, 0.0
    ).astype(BF)
    relay(3)
    for i in range(len(pieces)):
        core_copy(i).wait_recv()

    def residual(which):
        by_frame[:2] = jnp.zeros((2, CH, TOK), F32)
        bias = jnp.dot(w_all[2, :, PLANE:], ones[...], preferred_element_type=F32)
        by_frame[2] = jnp.transpose(lat[which, :, ds(x_hi * CH, CH)]).astype(F32) + bias

    residual(0)
    gain, shift = gain_ref[...], shift_ref[...]
    every("wait_recv", stat_copy)

    size = C // GROUPS
    total = jnp.sum(stats[...], axis=0)
    lane = lax.broadcasted_iota(jnp.int32, (8, C), 1)
    for hop in (1, 2, 4, 8):
        after = pltpu.roll(total, C - hop, 1)
        before = pltpu.roll(total, hop, 1)
        total = total + jnp.where(lax.rem(lane // hop, 2) == 0, after, before)
    total = total / (LEN * size)
    mean = total[0:1]
    var = total[1:2] - mean * mean
    moments[0] = jnp.where(line == 0, mean, jnp.where(line == 1, lax.rsqrt(var + 1e-06), 0.0))

    def to_beside(n, ref):
        return pltpu.make_async_remote_copy(
            src_ref=ref.at[0], dst_ref=ref.at[1], send_sem=b_send.at[n], recv_sem=b_recv.at[n],
            device_id=beside, device_id_type=MESH,
        )

    moments_copy = to_beside(1, moments)
    rims_copy = to_beside(2, rims)
    moments_copy.start()
    for n in range(len(RIMS)):
        rim_copy(n).wait_recv()
    rims_copy.start()

    def decode(which, tile):
        mean, inverse = moments[which, 0:1], moments[which, 1:2]

        def activate(x):
            return jax.nn.silu((x.astype(F32) - mean) * inverse * gain + shift)

        inner = activate(lat[which])
        for f in range(FRAMES):
            for h in range(TH):
                field[f * (TH + 2) + 1 + h, pl.ds(8, TW)] = inner[
                    (f * TH + h) * TW : (f * TH + h + 1) * TW
                ]

        row, column = tile // TILES, lax.rem(tile, TILES)
        above, below = row > 0, row < TILES - 1
        before, after = column > 0, column < TILES - 1
        inside = (
            above, below, before, after,
            above & before, above & after, below & before, below & after,
        )
        for n in range(len(RIMS)):
            rim = jnp.where(inside[n], activate(rims[which, rim_rows(n)]), 0.0)
            for f in range(FRAMES):
                first = f * (TH + 2)
                last = first + TH + 1
                if n < 2:
                    field[last if n else first, pl.ds(8, TW)] = rim[f * TW : (f + 1) * TW]
                elif n < 4:
                    for h in range(TH):
                        k = f * TH + h
                        field[first + h + 1, pl.ds(7 if n == 2 else 16, 1)] = rim[k : k + 1]
                else:
                    k = 4 * f + (3 if n < 6 else 0)
                    side = 7 if n in (4, 6) else 16
                    field[first if n < 6 else last, pl.ds(side, 1)] = rim[k : k + 1]

        if which:
            residual(which)

        def convolve(r, carry):
            x = jnp.concatenate(
                [
                    jnp.transpose(
                        jnp.concatenate(
                            [
                                field[r + (f * (TH + 2) + h), pl.ds(7 + s, TW)]
                                for f in range(FRAMES)
                                for h in range(TH)
                            ],
                            axis=0,
                        ).astype(BF)
                    )
                    for s in range(3)
                ],
                axis=0,
            )
            w = w_all[:, :, ds(r * 3 * C, 3 * C)].reshape(3 * CH, 3 * C)
            part = jnp.dot(w, x, preferred_element_type=F32)
            by_frame[...] += part.reshape(3, CH, TOK)
            return carry

        lax.fori_loop(0, 3, convolve, 0)
        at = lax.broadcasted_iota(jnp.int32, (CH, TOK), 1)
        frame = TH * TW
        one = jnp.where(at >= frame, pltpu.roll(by_frame[1], frame, 1), 0.0)
        two = jnp.where(at >= 2 * frame, pltpu.roll(by_frame[0], 2 * frame, 1), 0.0)
        out_t[which] = (by_frame[2] + one + two).astype(BF)

    def y_copy(t):
        theirs, hop = t // Z, lax.rem(t, Z)
        video = lax.rem(rep + theirs * Z, N)
        return pltpu.make_async_remote_copy(
            src_ref=out_t.at[theirs, ds(lax.rem(z + hop, Z) * CO, CO)], dst_ref=gathered.at[video],
            send_sem=y_send.at[t], recv_sem=y_recv.at[t],
            device_id={"seq": me + theirs * (twin - me), "rep": along_z(hop)},
            device_id_type=MESH,
        )

    decode(0, me)
    every("start", y_copy, 1, Z)
    gathered[rep] = out_t[0, ds(z * CO, CO)]
    lat_copy.wait_recv()
    moments_copy.wait_recv()
    rims_copy.wait_recv()
    decode(1, twin)
    every("start", y_copy, Z, N)
    for i in range(len(pieces)):
        w_copy(i).wait_send()
        core_copy(i).wait_send()
    for n in range(len(RIMS)):
        rim_copy(n).wait_send()
    lat_copy.wait_send()
    moments_copy.wait_send()
    rims_copy.wait_send()
    every("wait_send", k_copy)
    every("wait_send", v_copy)
    every("wait_send", q_copy)
    every("wait_send", o_copy)
    every("wait_send", stat_copy)
    every("wait_recv", y_copy)
    out_ref[...] = gathered[...]
    every("wait_send", y_copy)


def unit(q, k, v, taps, w_proj, gain, shift, bias):
    sem = pltpu.SemaphoreType.DMA
    vmem = pl.BlockSpec(memory_space=pltpu.VMEM)
    return pl.pallas_call(
        unit_kernel,
        out_shape=jax.ShapeDtypeStruct((N, CO, TOK), BF),
        in_specs=[pl.BlockSpec(memory_space=pl.ANY)] * 5 + [vmem] * 3,
        out_specs=vmem,
        scratch_shapes=[
            pltpu.VMEM((LEN, HD), BF),
            pltpu.VMEM((LEN, HD), BF),
            pltpu.VMEM((LEN, HD), BF),
            pltpu.VMEM((LEN, HD), F32),
            pltpu.VMEM((N, TOK, HD), BF),
            pltpu.VMEM((N, TOK, HD), BF),
            pltpu.VMEM((N, TOK, HD), BF),
            pltpu.VMEM((LEN, HD), BF),
            pltpu.VMEM((LEN, HD), BF),
            pltpu.VMEM((LEN, HD), BF),
            pltpu.VMEM((HD + EXTRA, LEN), BF),
            pltpu.VMEM((LEN, BQ), F32),
            pltpu.VMEM((LEN, BQ), F32),
            pltpu.VMEM((8, BQ), F32),
            pltpu.VMEM((HD, BQ), BF),
            pltpu.VMEM((HD + EXTRA, BQ), F32),
            pltpu.VMEM((LEN, HD), BF),
            pltpu.VMEM((TOK, N * HD), BF),
            pltpu.VMEM((N * HD, C), BF),
            pltpu.VMEM((3, CH, PLANE + 128), BF),
            pltpu.VMEM((2, TOK, C), BF),
            pltpu.VMEM((C // HD, TOK, HD), F32),
            pltpu.VMEM((RIM_ROWS, C), BF),
            pltpu.VMEM((2, RIM_ROWS, C), BF),
            pltpu.VMEM((8, C), F32),
            pltpu.VMEM((N, 8, C), F32),
            pltpu.VMEM((2, 8, C), F32),
            pltpu.VMEM((FRAMES * (TH + 2), PITCH, C), F32),
            pltpu.VMEM((128, TOK), BF),
            pltpu.VMEM((3, CH, TOK), F32),
            pltpu.VMEM((2, CH, TOK), BF),
            pltpu.VMEM((N, CO, TOK), BF),
        ]
        + [sem((N,))] * 8
        + [sem((4,)), sem((TAPS,))]
        + [sem((7,))] * 4
        + [sem((len(RIMS),))] * 2
        + [sem((N,))] * 2
        + [sem((3,))] * 2
        + [sem((N,))] * 2,
        compiler_params=pltpu.CompilerParams(
            collective_id=0, has_side_effects=True, vmem_limit_bytes=62 * 2**20
        ),
        cost_estimate=pl.CostEstimate(
            flops=4 * LEN * LEN * HD + 2 * TOK * TAPS * C * C,
            bytes_accessed=8 * 2**20,
            transcendentals=LEN * LEN,
        ),
        name="unit",
    )(q, k, v, taps, w_proj, gain, shift, bias)


def shards(queries, keys, values, w_proj, norm_gain, norm_bias, conv_weight, conv_bias):
    taps = conv_weight.reshape(TAPS, C, CO).transpose(0, 2, 1)
    q, k, v = (a.reshape(LEN, HD) for a in (queries, keys, values))
    out = unit(
        q, k, v, taps, w_proj, norm_gain[None], norm_bias[None], conv_bias[None]
    )
    return out.transpose(0, 2, 1).reshape(N, 1, FRAMES, TH, TW, CO)


def solution(mesh):
    return jax.shard_map(
        shards,
        mesh=mesh,
        in_specs=(
            P("rep", "seq", None, None),
            P("rep", "seq", None, None),
            P("rep", "seq", None, None),
            P(),
            P(),
            P(),
            P(None, None, None, None, "rep"),
            P("rep"),
        ),
        out_specs=P(None, "seq", None, None, None, "rep"),
        check_vma=False,
    )
```

```python
import math

import jax
import jax.numpy as jnp
from jax import lax
from jax.experimental import pallas as pl
from jax.experimental.pallas import tpu as pltpu
from jax.sharding import PartitionSpec as P

GROUPS = 32
FRAMES = 4
TH = 8
TW = 8
TILES = 4
HD = 128
N = 16
Z = 8
TOK = 256
LEN = N * TOK
C = 512
CO = C // N
HALF = CO // 2
TAPS = 27
PLANE = 9 * C
BQ = 512
BK = 512
EXTRA = 16
STEPS = LEN // BQ
PITCH = 24
BF = jnp.bfloat16
F32 = jnp.float32
MESH = pl.DeviceIdType.MESH
CORNERS = 4 * FRAMES * TW
RIMS = (
    (32, 32, 1, 0), (0, 32, -1, 0), (96, 32, 0, 1), (64, 32, 0, -1),
    (CORNERS + 48, 16, 1, 1), (CORNERS + 32, 16, 1, -1), (CORNERS + 16, 16, -1, 1), (CORNERS, 16, -1, -1),
)
RIM_ROWS = CORNERS + 4 * 16
CH = C // 2


def unit_kernel(
    q_ref, k_ref, v_ref, taps_ref, wp_ref, gain_ref, shift_ref, bias_ref, out_ref,
    q_raw, k_raw, v_raw, by_token, q_out, k_out, v_out,
    q_all, k_all, v_all, v_t, s_even, s_odd, m_buf, q_t, acc, o_buf, att, wp,
    w_all, lat, by_lanes, edges, rims, stat, stats, moments, field, ones, by_frame, out_t, gathered,
    q_send, q_recv, k_send, k_recv, v_send, v_recv, o_send, o_recv,
    raw_in, w_own, w_send, w_recv, c_send, c_recv, e_send, e_recv, t_send, t_recv, b_send, b_recv, y_send, y_recv,
):
    me = lax.axis_index("seq")
    rep = lax.axis_index("rep")
    x_hi = rep // Z
    z = lax.rem(rep, Z)
    half = lax.rem(me, 2)
    other_core = me + 1 - 2 * half
    twin = me + 2 - 4 * lax.rem(me // 2, 2)
    beside = {"seq": twin, "rep": lax.rem(rep + Z, N)}

    def along_z(d):
        return x_hi * Z + lax.rem(z + d + Z, Z)

    barrier = pltpu.get_barrier_semaphore()

    def greet(t, carry):
        pl.semaphore_signal(
            barrier, inc=1, device_id={"seq": lax.rem(me + t, N)}, device_id_type=MESH
        )
        return carry

    def greet_z(t, carry):
        for seq in (me, twin):
            pl.semaphore_signal(
                barrier, inc=1, device_id={"seq": seq, "rep": along_z(t)}, device_id_type=MESH
            )
        return carry

    lax.fori_loop(1, N, greet, 0)
    lax.fori_loop(1, Z, greet_z, 0)
    pl.semaphore_signal(barrier, inc=1, device_id=beside, device_id_type=MESH)

    k_in = pltpu.make_async_copy(k_ref, k_raw, raw_in.at[0])
    v_in = pltpu.make_async_copy(v_ref, v_raw, raw_in.at[1])
    q_in = pltpu.make_async_copy(q_ref, q_raw, raw_in.at[2])
    wp_in = pltpu.make_async_copy(wp_ref, wp, raw_in.at[3])
    k_in.start()
    v_in.start()
    q_in.start()
    wp_in.start()

    def ds(start, size):
        return pl.ds(pl.multiple_of(start, size), size)

    def own_tap(t):
        return pltpu.make_async_copy(
            taps_ref.at[t],
            w_all.at[t // 9, ds(z * CO, CO), ds(lax.rem(t, 9) * C, C)],
            w_own.at[t],
        )

    def tap_start(t, carry):
        own_tap(t).start()
        return carry

    lax.fori_loop(0, TAPS, tap_start, 0)
    square = (CO, CO)
    on = lax.broadcasted_iota(jnp.int32, square, 0) == lax.broadcasted_iota(jnp.int32, square, 1)
    bias = jnp.sum(
        jnp.where(on, jnp.broadcast_to(bias_ref[...], square), 0.0), axis=1, keepdims=True
    )
    high = bias.astype(BF).astype(F32)
    middle = (bias - high).astype(BF).astype(F32)
    low = bias - high - middle
    lane = lax.broadcasted_iota(jnp.int32, (CO, HD), 1)
    nought = jnp.zeros((CO, HD), F32)
    parts = jnp.where(lane == 0, high, jnp.where(lane == 1, middle, jnp.where(lane == 2, low, nought)))
    w_all[0, ds(z * CO, CO), PLANE:] = nought.astype(BF)
    w_all[1, ds(z * CO, CO), PLANE:] = nought.astype(BF)
    w_all[2, ds(z * CO, CO), PLANE:] = parts.astype(BF)
    v_t[HD:] = jnp.ones((EXTRA, LEN), BF)

    def by_head(copy, raw, out):
        copy.wait()

        def widen(b, carry):
            by_token[ds(b * TOK, TOK)] = raw[ds(b * TOK, TOK)].astype(F32)
            return carry

        lax.fori_loop(0, N, widen, 0)
        for h in range(N):
            out[h] = by_token[pl.ds(h, TOK, stride=N)].astype(BF)

    by_head(k_in, k_raw, k_out)
    pl.semaphore_wait(barrier, N + 2 * (Z - 1))

    def k_copy(t):
        to = lax.rem(me + t, N)
        return pltpu.make_async_remote_copy(
            src_ref=k_out.at[to], dst_ref=k_all.at[ds(me * TOK, TOK)],
            send_sem=k_send.at[t], recv_sem=k_recv.at[t],
            device_id={"seq": to}, device_id_type=MESH,
        )

    def v_copy(t):
        to = lax.rem(me + t, N)
        return pltpu.make_async_remote_copy(
            src_ref=v_out.at[to], dst_ref=v_all.at[ds(me * TOK, TOK)],
            send_sem=v_send.at[t], recv_sem=v_recv.at[t],
            device_id={"seq": to}, device_id_type=MESH,
        )

    def q_copy(t):
        to = lax.rem(me - t + N, N)
        return pltpu.make_async_remote_copy(
            src_ref=q_out.at[to], dst_ref=q_all.at[ds(t * TOK, TOK)],
            send_sem=q_send.at[t], recv_sem=q_recv.at[t],
            device_id={"seq": to}, device_id_type=MESH,
        )

    def o_copy(t):
        to = lax.rem(me + t, N)
        return pltpu.make_async_remote_copy(
            src_ref=o_buf.at[ds(t * TOK, TOK)], dst_ref=att.at[:, ds(me * HD, HD)],
            send_sem=o_send.at[t], recv_sem=o_recv.at[t],
            device_id={"seq": to}, device_id_type=MESH,
        )

    def every(act, copy, first=1, last=N):
        def body(t, carry):
            getattr(copy(t), act)()
            return carry
        lax.fori_loop(first, last, body, 0)

    pieces = [(-d, 1) for d in (1, 2, 3, 4)] + [(d, -1) for d in (1, 2, 3)]

    def shard_rows(d):
        return ds(lax.rem(z + d + Z, Z) * CO + half * HALF, HALF)

    def w_copy(i):
        d, turn = pieces[i]
        held = shard_rows(d + turn)
        return pltpu.make_async_remote_copy(
            src_ref=w_all.at[:, held], dst_ref=w_all.at[:, held],
            send_sem=w_send.at[i], recv_sem=w_recv.at[i],
            device_id={"rep": along_z(turn)}, device_id_type=MESH,
        )

    def core_copy(i):
        held = shard_rows(pieces[i][0])
        return pltpu.make_async_remote_copy(
            src_ref=w_all.at[:, held], dst_ref=w_all.at[:, held],
            send_sem=c_send.at[i], recv_sem=c_recv.at[i],
            device_id={"seq": other_core}, device_id_type=MESH,
        )

    def relay(i, *onward):
        w_copy(i).wait_recv()
        for j in onward:
            w_copy(j).start()
        core_copy(i).start()

    every("start", k_copy)
    every("wait", own_tap, 0, TAPS)
    w_copy(0).start()
    w_copy(4).start()
    by_head(v_in, v_raw, v_out)
    every("start", v_copy)
    by_head(q_in, q_raw, q_out)
    every("start", q_copy)

    def flip(place, block):
        v_t[:HD, place] = jnp.transpose(block)

    mine = ds(me * TOK, TOK)
    k_all[mine] = k_out[me]
    flip(mine, v_out[me])
    q_all[:TOK] = q_out[me]
    every("wait_recv", k_copy)

    factor = HD ** (-0.5) * math.log2(math.e)

    def query_block(u):
        q_t[...] = jnp.transpose(q_all[ds(u * BQ, BQ)])

    def scores(s_buf, keys, top):
        s = jnp.dot(k_all[keys], q_t[...], preferred_element_type=F32)
        s_buf[keys] = s
        return jnp.maximum(top, jnp.max(s.reshape(BK // 8, 8, BQ), axis=0))

    lowest = jnp.full((8, BQ), -jnp.inf, F32)

    def settle(top):
        m_buf[...] = jnp.broadcast_to(jnp.max(top, axis=0, keepdims=True), (8, BQ))

    def exps(s_buf, keys, m):
        below = s_buf[keys].reshape(BK // 8, 8, BQ) - m[None]
        return jnp.exp2(below * factor).reshape(BK, BQ).astype(BF)

    def weigh(p, keys):
        acc[...] += jnp.dot(v_t[:, keys], p, preferred_element_type=F32)

    def emit(u):
        o = (acc[:HD] / acc[HD : HD + 1]).astype(BF)
        o_buf[ds(u * BQ, BQ)] = jnp.transpose(o)

    def step(u, now, then):
        if then is not None:
            q_copy(2 * u + 2).wait_recv()
            q_copy(2 * u + 3).wait_recv()
            query_block(u + 1)
        m = m_buf[...]
        acc[...] = jnp.zeros_like(acc)

        def chunk(c, top):
            keys = ds(c * BK, BK)
            p = exps(now, keys, m)
            if then is not None:
                top = scores(then, keys, top)
            weigh(p, keys)
            return top

        top = lax.fori_loop(0, LEN // BK, chunk, lowest, unroll=2)
        if then is not None:
            settle(top)
        emit(u)

    q_copy(1).wait_recv()
    query_block(0)
    settle(
        lax.fori_loop(
            0, LEN // BK, lambda c, top: scores(s_even, ds(c * BK, BK), top), lowest
        )
    )
    relay(0, 1)
    relay(4, 5)

    def v_arrive(t, carry):
        v_copy(t).wait_recv()
        place = ds(lax.rem(me - t + N, N) * TOK, TOK)
        flip(place, v_all[place])
        return carry

    lax.fori_loop(1, N, v_arrive, 0)
    relay(1, 2)
    relay(5, 6)

    def steps(i, carry):
        step(2 * i, s_even, s_odd)

        @pl.when(i > 0)
        def _():
            o_copy(4 * i).start()

        o_copy(4 * i + 1).start()

        step(2 * i + 1, s_odd, s_even)
        o_copy(4 * i + 2).start()
        o_copy(4 * i + 3).start()

        @pl.when(i == 0)
        def _():
            relay(2, 3)
            relay(6)

        @pl.when(i == 2)
        def _():
            relay(3)

        return carry

    lax.fori_loop(0, STEPS // 2 - 1, steps, 0)
    step(STEPS - 2, s_even, s_odd)
    o_copy(N - 4).start()
    o_copy(N - 3).start()
    step(STEPS - 1, s_odd, None)
    o_copy(N - 2).start()
    o_copy(N - 1).start()
    own_o = pltpu.make_async_copy(o_buf.at[pl.ds(0, TOK)], att.at[:, ds(me * HD, HD)], o_recv.at[0])
    own_o.start()
    own_o.wait()
    every("wait_recv", o_copy)

    wp_in.wait()
    latent = jnp.dot(att[...], wp[...], preferred_element_type=F32).astype(BF)
    wide = latent.astype(F32)
    line = lax.broadcasted_iota(jnp.int32, (8, C), 0)
    stat[...] = jnp.where(
        line == 0,
        jnp.sum(wide, axis=0, keepdims=True),
        jnp.where(line == 1, jnp.sum(wide * wide, axis=0, keepdims=True), 0.0),
    )

    def stat_copy(t):
        return pltpu.make_async_remote_copy(
            src_ref=stat, dst_ref=stats.at[me],
            send_sem=t_send.at[t], recv_sem=t_recv.at[t],
            device_id={"seq": lax.rem(me + t, N)}, device_id_type=MESH,
        )

    every("start", stat_copy)
    lat[0] = latent
    lat_copy = pltpu.make_async_remote_copy(
        src_ref=lat.at[0], dst_ref=lat.at[1], send_sem=b_send.at[0], recv_sem=b_recv.at[0],
        device_id=beside, device_id_type=MESH,
    )
    lat_copy.start()
    for f in range(FRAMES):
        first, last = f * TH * TW, (f + 1) * TH * TW - TW
        edges[pl.ds(f * TW, TW)] = wide[first : first + TW].astype(BF)
        edges[pl.ds((FRAMES + f) * TW, TW)] = wide[last : last + TW].astype(BF)
    for j in range(C // HD):
        lanes = pl.ds(j * HD, HD)
        by_lanes[j] = wide[:, j * HD : (j + 1) * HD]
        edges[pl.ds(64, 32), lanes] = by_lanes[j, pl.ds(0, FRAMES * TH, stride=TW)].astype(BF)
        edges[pl.ds(96, 32), lanes] = by_lanes[j, pl.ds(TW - 1, FRAMES * TH, stride=TW)].astype(BF)
        for n, start in enumerate((0, TW - 1, TW, 2 * TW - 1)):
            corner = by_lanes[j, pl.ds(start, 16, stride=2 * TW)]
            edges[pl.ds(CORNERS + 16 * n, 16), lanes] = corner.astype(BF)

    row, column = me // TILES, lax.rem(me, TILES)

    def rim_rows(n):
        return pl.ds(n * 32, 32) if n < 4 else pl.ds(CORNERS + (n - 4) * 16, 16)

    def rim_copy(n):
        at, size, down, right = RIMS[n]
        to = lax.rem(row + down + TILES, TILES) * TILES + lax.rem(column + right + TILES, TILES)
        return pltpu.make_async_remote_copy(
            src_ref=edges.at[pl.ds(at, size)], dst_ref=rims.at[0, rim_rows(n)],
            send_sem=e_send.at[n], recv_sem=e_recv.at[n],
            device_id={"seq": to}, device_id_type=MESH,
        )

    for n in range(len(RIMS)):
        rim_copy(n).start()
    stats[me] = stat[...]
    ones[...] = jnp.where(
        lax.broadcasted_iota(jnp.int32, (128, TOK), 0) < 3, 1.0, 0.0
    ).astype(BF)
    gain, shift = gain_ref[...], shift_ref[...]
    every("wait_recv", stat_copy)

    size = C // GROUPS
    total = jnp.sum(stats[...], axis=0)
    lane = lax.broadcasted_iota(jnp.int32, (8, C), 1)
    for hop in (1, 2, 4, 8):
        after = pltpu.roll(total, C - hop, 1)
        before = pltpu.roll(total, hop, 1)
        total = total + jnp.where(lax.rem(lane // hop, 2) == 0, after, before)
    total = total / (LEN * size)
    mean = total[0:1]
    var = total[1:2] - mean * mean
    moments[0] = jnp.where(line == 0, mean, jnp.where(line == 1, lax.rsqrt(var + 1e-06), 0.0))

    def to_beside(n, ref):
        return pltpu.make_async_remote_copy(
            src_ref=ref.at[0], dst_ref=ref.at[1], send_sem=b_send.at[n], recv_sem=b_recv.at[n],
            device_id=beside, device_id_type=MESH,
        )

    moments_copy = to_beside(1, moments)
    rims_copy = to_beside(2, rims)
    moments_copy.start()
    for n in range(len(RIMS)):
        rim_copy(n).wait_recv()
    rims_copy.start()

    def decode(which, tile):
        mean, inverse = moments[which, 0:1], moments[which, 1:2]

        def activate(x):
            return jax.nn.silu((x.astype(F32) - mean) * inverse * gain + shift)

        inner = activate(lat[which])
        for f in range(FRAMES):
            for h in range(TH):
                field[f * (TH + 2) + 1 + h, pl.ds(8, TW)] = inner[
                    (f * TH + h) * TW : (f * TH + h + 1) * TW
                ]

        row, column = tile // TILES, lax.rem(tile, TILES)
        above, below = row > 0, row < TILES - 1
        before, after = column > 0, column < TILES - 1
        inside = (
            above, below, before, after,
            above & before, above & after, below & before, below & after,
        )
        for n in range(len(RIMS)):
            rim = jnp.where(inside[n], activate(rims[which, rim_rows(n)]), 0.0)
            for f in range(FRAMES):
                first = f * (TH + 2)
                last = first + TH + 1
                if n < 2:
                    field[last if n else first, pl.ds(8, TW)] = rim[f * TW : (f + 1) * TW]
                elif n < 4:
                    for h in range(TH):
                        k = f * TH + h
                        field[first + h + 1, pl.ds(7 if n == 2 else 16, 1)] = rim[k : k + 1]
                else:
                    k = 4 * f + (3 if n < 6 else 0)
                    side = 7 if n in (4, 6) else 16
                    field[first if n < 6 else last, pl.ds(side, 1)] = rim[k : k + 1]

        if which == 0:
            for i in range(len(pieces)):
                core_copy(i).wait_recv()
        by_frame[:2] = jnp.zeros((2, CH, TOK), F32)
        by_frame[2] = jnp.transpose(lat[which, :, ds(x_hi * CH, CH)]).astype(F32) + jnp.dot(
            w_all[2, :, PLANE:], ones[...], preferred_element_type=F32
        )

        def convolve(r, carry):
            x = jnp.concatenate(
                [
                    jnp.transpose(
                        jnp.concatenate(
                            [
                                field[r + (f * (TH + 2) + h), pl.ds(7 + s, TW)]
                                for f in range(FRAMES)
                                for h in range(TH)
                            ],
                            axis=0,
                        ).astype(BF)
                    )
                    for s in range(3)
                ],
                axis=0,
            )
            w = w_all[:, :, ds(r * 3 * C, 3 * C)].reshape(3 * CH, 3 * C)
            part = jnp.dot(w, x, preferred_element_type=F32)
            by_frame[...] += part.reshape(3, CH, TOK)
            return carry

        lax.fori_loop(0, 3, convolve, 0)
        at = lax.broadcasted_iota(jnp.int32, (CH, TOK), 1)
        frame = TH * TW
        one = jnp.where(at >= frame, pltpu.roll(by_frame[1], frame, 1), 0.0)
        two = jnp.where(at >= 2 * frame, pltpu.roll(by_frame[0], 2 * frame, 1), 0.0)
        out_t[which] = (by_frame[2] + one + two).astype(BF)

    def y_copy(t):
        theirs, hop = t // Z, lax.rem(t, Z)
        video = lax.rem(rep + theirs * Z, N)
        return pltpu.make_async_remote_copy(
            src_ref=out_t.at[theirs, ds(lax.rem(z + hop, Z) * CO, CO)], dst_ref=gathered.at[video],
            send_sem=y_send.at[t], recv_sem=y_recv.at[t],
            device_id={"seq": me + theirs * (twin - me), "rep": along_z(hop)},
            device_id_type=MESH,
        )

    decode(0, me)
    every("start", y_copy, 1, Z)
    gathered[rep] = out_t[0, ds(z * CO, CO)]
    lat_copy.wait_recv()
    moments_copy.wait_recv()
    rims_copy.wait_recv()
    decode(1, twin)
    every("start", y_copy, Z, N)
    for i in range(len(pieces)):
        w_copy(i).wait_send()
        core_copy(i).wait_send()
    for n in range(len(RIMS)):
        rim_copy(n).wait_send()
    lat_copy.wait_send()
    moments_copy.wait_send()
    rims_copy.wait_send()
    every("wait_send", k_copy)
    every("wait_send", v_copy)
    every("wait_send", q_copy)
    every("wait_send", o_copy)
    every("wait_send", stat_copy)
    every("wait_recv", y_copy)
    out_ref[...] = gathered[...]
    every("wait_send", y_copy)


def unit(q, k, v, taps, w_proj, gain, shift, bias):
    sem = pltpu.SemaphoreType.DMA
    vmem = pl.BlockSpec(memory_space=pltpu.VMEM)
    return pl.pallas_call(
        unit_kernel,
        out_shape=jax.ShapeDtypeStruct((N, CO, TOK), BF),
        in_specs=[pl.BlockSpec(memory_space=pltpu.HBM)] * 5 + [vmem] * 3,
        out_specs=vmem,
        scratch_shapes=[
            pltpu.VMEM((LEN, HD), BF),
            pltpu.VMEM((LEN, HD), BF),
            pltpu.VMEM((LEN, HD), BF),
            pltpu.VMEM((LEN, HD), F32),
            pltpu.VMEM((N, TOK, HD), BF),
            pltpu.VMEM((N, TOK, HD), BF),
            pltpu.VMEM((N, TOK, HD), BF),
            pltpu.VMEM((LEN, HD), BF),
            pltpu.VMEM((LEN, HD), BF),
            pltpu.VMEM((LEN, HD), BF),
            pltpu.VMEM((HD + EXTRA, LEN), BF),
            pltpu.VMEM((LEN, BQ), F32),
            pltpu.VMEM((LEN, BQ), F32),
            pltpu.VMEM((8, BQ), F32),
            pltpu.VMEM((HD, BQ), BF),
            pltpu.VMEM((HD + EXTRA, BQ), F32),
            pltpu.VMEM((LEN, HD), BF),
            pltpu.VMEM((TOK, N * HD), BF),
            pltpu.VMEM((N * HD, C), BF),
            pltpu.VMEM((3, CH, PLANE + 128), BF),
            pltpu.VMEM((2, TOK, C), BF),
            pltpu.VMEM((C // HD, TOK, HD), F32),
            pltpu.VMEM((RIM_ROWS, C), BF),
            pltpu.VMEM((2, RIM_ROWS, C), BF),
            pltpu.VMEM((8, C), F32),
            pltpu.VMEM((N, 8, C), F32),
            pltpu.VMEM((2, 8, C), F32),
            pltpu.VMEM((FRAMES * (TH + 2), PITCH, C), F32),
            pltpu.VMEM((128, TOK), BF),
            pltpu.VMEM((3, CH, TOK), F32),
            pltpu.VMEM((2, CH, TOK), BF),
            pltpu.VMEM((N, CO, TOK), BF),
        ]
        + [sem((N,))] * 8
        + [sem((4,)), sem((TAPS,))]
        + [sem((7,))] * 4
        + [sem((len(RIMS),))] * 2
        + [sem((N,))] * 2
        + [sem((3,))] * 2
        + [sem((N,))] * 2,
        compiler_params=pltpu.CompilerParams(
            collective_id=0, has_side_effects=True, vmem_limit_bytes=53 * 2**20
        ),
        cost_estimate=pl.CostEstimate(
            flops=4 * LEN * LEN * HD + 2 * TOK * TAPS * C * C,
            bytes_accessed=8 * 2**20,
            transcendentals=LEN * LEN,
        ),
        name="unit",
    )(q, k, v, taps, w_proj, gain, shift, bias)


def shards(queries, keys, values, w_proj, norm_gain, norm_bias, conv_weight, conv_bias):
    taps = conv_weight.reshape(TAPS, C, CO).transpose(0, 2, 1)
    q, k, v = (a.reshape(LEN, HD) for a in (queries, keys, values))
    out = unit(
        q, k, v, taps, w_proj, norm_gain[None], norm_bias[None], conv_bias[None]
    )
    return out.transpose(0, 2, 1).reshape(N, 1, FRAMES, TH, TW, CO)


def solution(mesh):
    return jax.shard_map(
        shards,
        mesh=mesh,
        in_specs=(
            P("rep", "seq", None, None),
            P("rep", "seq", None, None),
            P("rep", "seq", None, None),
            P(),
            P(),
            P(),
            P(None, None, None, None, "rep"),
            P("rep"),
        ),
        out_specs=P(None, "seq", None, None, None, "rep"),
        check_vma=False,
    )
```

```python
import math

import jax
import jax.numpy as jnp
from jax import lax
from jax.experimental import pallas as pl
from jax.experimental.pallas import tpu as pltpu
from jax.sharding import PartitionSpec as P

GROUPS = 32
FRAMES = 4
TH = 8
TW = 8
TILES = 4
HD = 128
N = 16
Z = 8
TOK = 256
LEN = N * TOK
C = 512
CO = C // N
HALF = CO // 2
TAPS = 27
PLANE = 9 * C
BQ = 512
BK = 512
EXTRA = 16
STEPS = LEN // BQ
PITCH = 24
BF = jnp.bfloat16
F32 = jnp.float32
MESH = pl.DeviceIdType.MESH
CORNERS = 4 * FRAMES * TW
RIMS = (
    (32, 32, 1, 0), (0, 32, -1, 0), (96, 32, 0, 1), (64, 32, 0, -1),
    (CORNERS + 48, 16, 1, 1), (CORNERS + 32, 16, 1, -1), (CORNERS + 16, 16, -1, 1), (CORNERS, 16, -1, -1),
)
RIM_ROWS = CORNERS + 4 * 16
CH = C // 2


def unit_kernel(
    q_ref, k_ref, v_ref, taps_ref, wp_ref, gain_ref, shift_ref, bias_ref, out_ref,
    q_raw, k_raw, v_raw, by_token, q_out, k_out, v_out,
    q_all, k_all, v_all, v_t, s_even, s_odd, m_buf, q_t, acc, o_buf, att, wp,
    w_all, lat, by_lanes, edges, rims, stat, stats, moments, field, ones, by_frame, out_t, gathered,
    q_send, q_recv, k_send, k_recv, v_send, v_recv, o_send, o_recv,
    raw_in, w_own, w_send, w_recv, c_send, c_recv, e_send, e_recv, t_send, t_recv, b_send, b_recv, y_send, y_recv,
):
    me = lax.axis_index("seq")
    rep = lax.axis_index("rep")
    x_hi = rep // Z
    z = lax.rem(rep, Z)
    half = lax.rem(me, 2)
    other_core = me + 1 - 2 * half
    twin = me + 2 - 4 * lax.rem(me // 2, 2)
    beside = {"seq": twin, "rep": lax.rem(rep + Z, N)}

    def along_z(d):
        return x_hi * Z + lax.rem(z + d + Z, Z)

    barrier = pltpu.get_barrier_semaphore()

    def greet(t, carry):
        pl.semaphore_signal(
            barrier, inc=1, device_id={"seq": lax.rem(me + t, N)}, device_id_type=MESH
        )
        return carry

    def greet_z(t, carry):
        for seq in (me, twin):
            pl.semaphore_signal(
                barrier, inc=1, device_id={"seq": seq, "rep": along_z(t)}, device_id_type=MESH
            )
        return carry

    lax.fori_loop(1, N, greet, 0)
    lax.fori_loop(1, Z, greet_z, 0)
    pl.semaphore_signal(barrier, inc=1, device_id=beside, device_id_type=MESH)

    k_in = pltpu.make_async_copy(k_ref, k_raw, raw_in.at[0])
    v_in = pltpu.make_async_copy(v_ref, v_raw, raw_in.at[1])
    q_in = pltpu.make_async_copy(q_ref, q_raw, raw_in.at[2])
    wp_in = pltpu.make_async_copy(wp_ref, wp, raw_in.at[3])
    k_in.start()
    v_in.start()
    q_in.start()
    wp_in.start()

    def ds(start, size):
        return pl.ds(pl.multiple_of(start, size), size)

    def own_tap(t):
        return pltpu.make_async_copy(
            taps_ref.at[t],
            w_all.at[t // 9, ds(z * CO, CO), ds(lax.rem(t, 9) * C, C)],
            w_own.at[t],
        )

    def tap_start(t, carry):
        own_tap(t).start()
        return carry

    lax.fori_loop(0, TAPS, tap_start, 0)
    square = (CO, CO)
    on = lax.broadcasted_iota(jnp.int32, square, 0) == lax.broadcasted_iota(jnp.int32, square, 1)
    bias = jnp.sum(
        jnp.where(on, jnp.broadcast_to(bias_ref[...], square), 0.0), axis=1, keepdims=True
    )
    high = bias.astype(BF).astype(F32)
    middle = (bias - high).astype(BF).astype(F32)
    low = bias - high - middle
    lane = lax.broadcasted_iota(jnp.int32, (CO, HD), 1)
    nought = jnp.zeros((CO, HD), F32)
    parts = jnp.where(lane == 0, high, jnp.where(lane == 1, middle, jnp.where(lane == 2, low, nought)))
    w_all[0, ds(z * CO, CO), PLANE:] = nought.astype(BF)
    w_all[1, ds(z * CO, CO), PLANE:] = nought.astype(BF)
    w_all[2, ds(z * CO, CO), PLANE:] = parts.astype(BF)
    v_t[HD:] = jnp.ones((EXTRA, LEN), BF)

    def by_head(copy, raw, out):
        copy.wait()

        def widen(b, carry):
            by_token[ds(b * TOK, TOK)] = raw[ds(b * TOK, TOK)].astype(F32)
            return carry

        lax.fori_loop(0, N, widen, 0)
        for h in range(N):
            out[h] = by_token[pl.ds(h, TOK, stride=N)].astype(BF)

    by_head(k_in, k_raw, k_out)
    pl.semaphore_wait(barrier, N + 2 * (Z - 1))

    def k_copy(t):
        to = lax.rem(me + t, N)
        return pltpu.make_async_remote_copy(
            src_ref=k_out.at[to], dst_ref=k_all.at[ds(me * TOK, TOK)],
            send_sem=k_send.at[t], recv_sem=k_recv.at[t],
            device_id={"seq": to}, device_id_type=MESH,
        )

    def v_copy(t):
        to = lax.rem(me + t, N)
        return pltpu.make_async_remote_copy(
            src_ref=v_out.at[to], dst_ref=v_all.at[ds(me * TOK, TOK)],
            send_sem=v_send.at[t], recv_sem=v_recv.at[t],
            device_id={"seq": to}, device_id_type=MESH,
        )

    def q_copy(t):
        to = lax.rem(me - t + N, N)
        return pltpu.make_async_remote_copy(
            src_ref=q_out.at[to], dst_ref=q_all.at[ds(t * TOK, TOK)],
            send_sem=q_send.at[t], recv_sem=q_recv.at[t],
            device_id={"seq": to}, device_id_type=MESH,
        )

    def o_copy(t):
        to = lax.rem(me + t, N)
        return pltpu.make_async_remote_copy(
            src_ref=o_buf.at[ds(t * TOK, TOK)], dst_ref=att.at[:, ds(me * HD, HD)],
            send_sem=o_send.at[t], recv_sem=o_recv.at[t],
            device_id={"seq": to}, device_id_type=MESH,
        )

    def every(act, copy, first=1, last=N):
        def body(t, carry):
            getattr(copy(t), act)()
            return carry
        lax.fori_loop(first, last, body, 0)

    pieces = [(-d, 1) for d in (1, 2, 3, 4)] + [(d, -1) for d in (1, 2, 3)]

    def shard_rows(d):
        return ds(lax.rem(z + d + Z, Z) * CO + half * HALF, HALF)

    def w_copy(i):
        d, turn = pieces[i]
        held = shard_rows(d + turn)
        return pltpu.make_async_remote_copy(
            src_ref=w_all.at[:, held], dst_ref=w_all.at[:, held],
            send_sem=w_send.at[i], recv_sem=w_recv.at[i],
            device_id={"rep": along_z(turn)}, device_id_type=MESH,
        )

    def core_copy(i):
        held = shard_rows(pieces[i][0])
        return pltpu.make_async_remote_copy(
            src_ref=w_all.at[:, held], dst_ref=w_all.at[:, held],
            send_sem=c_send.at[i], recv_sem=c_recv.at[i],
            device_id={"seq": other_core}, device_id_type=MESH,
        )

    def relay(i, *onward):
        w_copy(i).wait_recv()
        for j in onward:
            w_copy(j).start()
        core_copy(i).start()

    every("start", k_copy)
    every("wait", own_tap, 0, TAPS)
    w_copy(0).start()
    by_head(v_in, v_raw, v_out)
    every("start", v_copy)
    w_copy(4).start()
    by_head(q_in, q_raw, q_out)
    every("start", q_copy)

    def flip(place, block):
        v_t[:HD, place] = jnp.transpose(block)

    mine = ds(me * TOK, TOK)
    k_all[mine] = k_out[me]
    flip(mine, v_out[me])
    q_all[:TOK] = q_out[me]
    every("wait_recv", k_copy)

    factor = HD ** (-0.5) * math.log2(math.e)

    def query_block(u):
        q_t[...] = jnp.transpose(q_all[ds(u * BQ, BQ)])

    def scores(s_buf, keys, top):
        s = jnp.dot(k_all[keys], q_t[...], preferred_element_type=F32)
        s_buf[keys] = s
        return jnp.maximum(top, jnp.max(s.reshape(BK // 8, 8, BQ), axis=0))

    lowest = jnp.full((8, BQ), -jnp.inf, F32)

    def settle(top):
        m_buf[...] = jnp.broadcast_to(jnp.max(top, axis=0, keepdims=True), (8, BQ))

    def exps(s_buf, keys, m):
        below = s_buf[keys].reshape(BK // 8, 8, BQ) - m[None]
        return jnp.exp2(below * factor).reshape(BK, BQ).astype(BF)

    def weigh(p, keys):
        acc[...] += jnp.dot(v_t[:, keys], p, preferred_element_type=F32)

    def emit(u):
        o = (acc[:HD] / acc[HD : HD + 1]).astype(BF)
        o_buf[ds(u * BQ, BQ)] = jnp.transpose(o)

    def step(u, now, then):
        if then is not None:
            q_copy(2 * u + 2).wait_recv()
            q_copy(2 * u + 3).wait_recv()
            query_block(u + 1)
        m = m_buf[...]
        acc[...] = jnp.zeros_like(acc)

        def chunk(c, top):
            keys = ds(c * BK, BK)
            p = exps(now, keys, m)
            if then is not None:
                top = scores(then, keys, top)
            weigh(p, keys)
            return top

        top = lax.fori_loop(0, LEN // BK, chunk, lowest, unroll=2)
        if then is not None:
            settle(top)
        emit(u)

    q_copy(1).wait_recv()
    query_block(0)
    settle(
        lax.fori_loop(
            0, LEN // BK, lambda c, top: scores(s_even, ds(c * BK, BK), top), lowest
        )
    )
    relay(0, 1)

    def v_arrive(t, carry):
        v_copy(t).wait_recv()
        place = ds(lax.rem(me - t + N, N) * TOK, TOK)
        flip(place, v_all[place])
        return carry

    lax.fori_loop(1, N, v_arrive, 0)
    relay(1, 2)
    relay(4, 5)

    def steps(i, carry):
        step(2 * i, s_even, s_odd)

        @pl.when(i > 0)
        def _():
            o_copy(4 * i).start()

        o_copy(4 * i + 1).start()

        step(2 * i + 1, s_odd, s_even)
        o_copy(4 * i + 2).start()
        o_copy(4 * i + 3).start()

        @pl.when(i == 0)
        def _():
            relay(2, 3)
            relay(5, 6)

        @pl.when(i == 2)
        def _():
            relay(3)
            relay(6)

        return carry

    lax.fori_loop(0, STEPS // 2 - 1, steps, 0)
    step(STEPS - 2, s_even, s_odd)
    o_copy(N - 4).start()
    o_copy(N - 3).start()
    step(STEPS - 1, s_odd, None)
    o_copy(N - 2).start()
    o_copy(N - 1).start()
    own_o = pltpu.make_async_copy(o_buf.at[pl.ds(0, TOK)], att.at[:, ds(me * HD, HD)], o_recv.at[0])
    own_o.start()
    own_o.wait()
    every("wait_recv", o_copy)

    wp_in.wait()
    latent = jnp.dot(att[...], wp[...], preferred_element_type=F32).astype(BF)
    wide = latent.astype(F32)
    line = lax.broadcasted_iota(jnp.int32, (8, C), 0)
    stat[...] = jnp.where(
        line == 0,
        jnp.sum(wide, axis=0, keepdims=True),
        jnp.where(line == 1, jnp.sum(wide * wide, axis=0, keepdims=True), 0.0),
    )

    def stat_copy(t):
        return pltpu.make_async_remote_copy(
            src_ref=stat, dst_ref=stats.at[me],
            send_sem=t_send.at[t], recv_sem=t_recv.at[t],
            device_id={"seq": lax.rem(me + t, N)}, device_id_type=MESH,
        )

    every("start", stat_copy)
    lat[0] = latent
    lat_copy = pltpu.make_async_remote_copy(
        src_ref=lat.at[0], dst_ref=lat.at[1], send_sem=b_send.at[0], recv_sem=b_recv.at[0],
        device_id=beside, device_id_type=MESH,
    )
    lat_copy.start()
    for f in range(FRAMES):
        first, last = f * TH * TW, (f + 1) * TH * TW - TW
        edges[pl.ds(f * TW, TW)] = wide[first : first + TW].astype(BF)
        edges[pl.ds((FRAMES + f) * TW, TW)] = wide[last : last + TW].astype(BF)
    for j in range(C // HD):
        lanes = pl.ds(j * HD, HD)
        by_lanes[j] = wide[:, j * HD : (j + 1) * HD]
        edges[pl.ds(64, 32), lanes] = by_lanes[j, pl.ds(0, FRAMES * TH, stride=TW)].astype(BF)
        edges[pl.ds(96, 32), lanes] = by_lanes[j, pl.ds(TW - 1, FRAMES * TH, stride=TW)].astype(BF)
        for n, start in enumerate((0, TW - 1, TW, 2 * TW - 1)):
            corner = by_lanes[j, pl.ds(start, 16, stride=2 * TW)]
            edges[pl.ds(CORNERS + 16 * n, 16), lanes] = corner.astype(BF)

    row, column = me // TILES, lax.rem(me, TILES)

    def rim_rows(n):
        return pl.ds(n * 32, 32) if n < 4 else pl.ds(CORNERS + (n - 4) * 16, 16)

    def rim_copy(n):
        at, size, down, right = RIMS[n]
        to = lax.rem(row + down + TILES, TILES) * TILES + lax.rem(column + right + TILES, TILES)
        return pltpu.make_async_remote_copy(
            src_ref=edges.at[pl.ds(at, size)], dst_ref=rims.at[0, rim_rows(n)],
            send_sem=e_send.at[n], recv_sem=e_recv.at[n],
            device_id={"seq": to}, device_id_type=MESH,
        )

    for n in range(len(RIMS)):
        rim_copy(n).start()
    stats[me] = stat[...]
    ones[...] = jnp.where(
        lax.broadcasted_iota(jnp.int32, (128, TOK), 0) < 3, 1.0, 0.0
    ).astype(BF)
    gain, shift = gain_ref[...], shift_ref[...]
    every("wait_recv", stat_copy)

    size = C // GROUPS
    total = jnp.sum(stats[...], axis=0)
    lane = lax.broadcasted_iota(jnp.int32, (8, C), 1)
    for hop in (1, 2, 4, 8):
        after = pltpu.roll(total, C - hop, 1)
        before = pltpu.roll(total, hop, 1)
        total = total + jnp.where(lax.rem(lane // hop, 2) == 0, after, before)
    total = total / (LEN * size)
    mean = total[0:1]
    var = total[1:2] - mean * mean
    moments[0] = jnp.where(line == 0, mean, jnp.where(line == 1, lax.rsqrt(var + 1e-06), 0.0))

    def to_beside(n, ref):
        return pltpu.make_async_remote_copy(
            src_ref=ref.at[0], dst_ref=ref.at[1], send_sem=b_send.at[n], recv_sem=b_recv.at[n],
            device_id=beside, device_id_type=MESH,
        )

    moments_copy = to_beside(1, moments)
    rims_copy = to_beside(2, rims)
    moments_copy.start()
    for n in range(len(RIMS)):
        rim_copy(n).wait_recv()
    rims_copy.start()

    def decode(which, tile):
        mean, inverse = moments[which, 0:1], moments[which, 1:2]

        def activate(x):
            return jax.nn.silu((x.astype(F32) - mean) * inverse * gain + shift)

        inner = activate(lat[which])
        for f in range(FRAMES):
            for h in range(TH):
                field[f * (TH + 2) + 1 + h, pl.ds(8, TW)] = inner[
                    (f * TH + h) * TW : (f * TH + h + 1) * TW
                ]

        row, column = tile // TILES, lax.rem(tile, TILES)
        above, below = row > 0, row < TILES - 1
        before, after = column > 0, column < TILES - 1
        inside = (
            above, below, before, after,
            above & before, above & after, below & before, below & after,
        )
        for n in range(len(RIMS)):
            rim = jnp.where(inside[n], activate(rims[which, rim_rows(n)]), 0.0)
            for f in range(FRAMES):
                first = f * (TH + 2)
                last = first + TH + 1
                if n < 2:
                    field[last if n else first, pl.ds(8, TW)] = rim[f * TW : (f + 1) * TW]
                elif n < 4:
                    for h in range(TH):
                        k = f * TH + h
                        field[first + h + 1, pl.ds(7 if n == 2 else 16, 1)] = rim[k : k + 1]
                else:
                    k = 4 * f + (3 if n < 6 else 0)
                    side = 7 if n in (4, 6) else 16
                    field[first if n < 6 else last, pl.ds(side, 1)] = rim[k : k + 1]

        if which == 0:
            for i in range(len(pieces)):
                core_copy(i).wait_recv()
        by_frame[:2] = jnp.zeros((2, CH, TOK), F32)
        by_frame[2] = jnp.transpose(lat[which, :, ds(x_hi * CH, CH)]).astype(F32) + jnp.dot(
            w_all[2, :, PLANE:], ones[...], preferred_element_type=F32
        )

        def convolve(r, carry):
            x = jnp.concatenate(
                [
                    jnp.transpose(
                        jnp.concatenate(
                            [
                                field[r + (f * (TH + 2) + h), pl.ds(7 + s, TW)]
                                for f in range(FRAMES)
                                for h in range(TH)
                            ],
                            axis=0,
                        ).astype(BF)
                    )
                    for s in range(3)
                ],
                axis=0,
            )
            w = w_all[:, :, ds(r * 3 * C, 3 * C)].reshape(3 * CH, 3 * C)
            part = jnp.dot(w, x, preferred_element_type=F32)
            by_frame[...] += part.reshape(3, CH, TOK)
            return carry

        lax.fori_loop(0, 3, convolve, 0)
        at = lax.broadcasted_iota(jnp.int32, (CH, TOK), 1)
        frame = TH * TW
        one = jnp.where(at >= frame, pltpu.roll(by_frame[1], frame, 1), 0.0)
        two = jnp.where(at >= 2 * frame, pltpu.roll(by_frame[0], 2 * frame, 1), 0.0)
        out_t[which] = (by_frame[2] + one + two).astype(BF)

    def y_copy(t):
        theirs, hop = t // Z, lax.rem(t, Z)
        video = lax.rem(rep + theirs * Z, N)
        return pltpu.make_async_remote_copy(
            src_ref=out_t.at[theirs, ds(lax.rem(z + hop, Z) * CO, CO)], dst_ref=gathered.at[video],
            send_sem=y_send.at[t], recv_sem=y_recv.at[t],
            device_id={"seq": me + theirs * (twin - me), "rep": along_z(hop)},
            device_id_type=MESH,
        )

    decode(0, me)
    every("start", y_copy, 1, Z)
    gathered[rep] = out_t[0, ds(z * CO, CO)]
    lat_copy.wait_recv()
    moments_copy.wait_recv()
    rims_copy.wait_recv()
    decode(1, twin)
    every("start", y_copy, Z, N)
    for i in range(len(pieces)):
        w_copy(i).wait_send()
        core_copy(i).wait_send()
    for n in range(len(RIMS)):
        rim_copy(n).wait_send()
    lat_copy.wait_send()
    moments_copy.wait_send()
    rims_copy.wait_send()
    every("wait_send", k_copy)
    every("wait_send", v_copy)
    every("wait_send", q_copy)
    every("wait_send", o_copy)
    every("wait_send", stat_copy)
    every("wait_recv", y_copy)
    out_ref[...] = gathered[...]
    every("wait_send", y_copy)


def unit(q, k, v, taps, w_proj, gain, shift, bias):
    sem = pltpu.SemaphoreType.DMA
    vmem = pl.BlockSpec(memory_space=pltpu.VMEM)
    return pl.pallas_call(
        unit_kernel,
        out_shape=jax.ShapeDtypeStruct((N, CO, TOK), BF),
        in_specs=[pl.BlockSpec(memory_space=pl.ANY)] * 5 + [vmem] * 3,
        out_specs=vmem,
        scratch_shapes=[
            pltpu.VMEM((LEN, HD), BF),
            pltpu.VMEM((LEN, HD), BF),
            pltpu.VMEM((LEN, HD), BF),
            pltpu.VMEM((LEN, HD), F32),
            pltpu.VMEM((N, TOK, HD), BF),
            pltpu.VMEM((N, TOK, HD), BF),
            pltpu.VMEM((N, TOK, HD), BF),
            pltpu.VMEM((LEN, HD), BF),
            pltpu.VMEM((LEN, HD), BF),
            pltpu.VMEM((LEN, HD), BF),
            pltpu.VMEM((HD + EXTRA, LEN), BF),
            pltpu.VMEM((LEN, BQ), F32),
            pltpu.VMEM((LEN, BQ), F32),
            pltpu.VMEM((8, BQ), F32),
            pltpu.VMEM((HD, BQ), BF),
            pltpu.VMEM((HD + EXTRA, BQ), F32),
            pltpu.VMEM((LEN, HD), BF),
            pltpu.VMEM((TOK, N * HD), BF),
            pltpu.VMEM((N * HD, C), BF),
            pltpu.VMEM((3, CH, PLANE + 128), BF),
            pltpu.VMEM((2, TOK, C), BF),
            pltpu.VMEM((C // HD, TOK, HD), F32),
            pltpu.VMEM((RIM_ROWS, C), BF),
            pltpu.VMEM((2, RIM_ROWS, C), BF),
            pltpu.VMEM((8, C), F32),
            pltpu.VMEM((N, 8, C), F32),
            pltpu.VMEM((2, 8, C), F32),
            pltpu.VMEM((FRAMES * (TH + 2), PITCH, C), F32),
            pltpu.VMEM((128, TOK), BF),
            pltpu.VMEM((3, CH, TOK), F32),
            pltpu.VMEM((2, CH, TOK), BF),
            pltpu.VMEM((N, CO, TOK), BF),
        ]
        + [sem((N,))] * 8
        + [sem((4,)), sem((TAPS,))]
        + [sem((7,))] * 4
        + [sem((len(RIMS),))] * 2
        + [sem((N,))] * 2
        + [sem((3,))] * 2
        + [sem((N,))] * 2,
        compiler_params=pltpu.CompilerParams(
            collective_id=0, has_side_effects=True, vmem_limit_bytes=62 * 2**20
        ),
        cost_estimate=pl.CostEstimate(
            flops=4 * LEN * LEN * HD + 2 * TOK * TAPS * C * C,
            bytes_accessed=8 * 2**20,
            transcendentals=LEN * LEN,
        ),
        name="unit",
    )(q, k, v, taps, w_proj, gain, shift, bias)


def shards(queries, keys, values, w_proj, norm_gain, norm_bias, conv_weight, conv_bias):
    taps = conv_weight.reshape(TAPS, C, CO).transpose(0, 2, 1)
    q, k, v = (a.reshape(LEN, HD) for a in (queries, keys, values))
    out = unit(
        q, k, v, taps, w_proj, norm_gain[None], norm_bias[None], conv_bias[None]
    )
    return out.transpose(0, 2, 1).reshape(N, 1, FRAMES, TH, TW, CO)


def solution(mesh):
    return jax.shard_map(
        shards,
        mesh=mesh,
        in_specs=(
            P("rep", "seq", None, None),
            P("rep", "seq", None, None),
            P("rep", "seq", None, None),
            P(),
            P(),
            P(),
            P(None, None, None, None, "rep"),
            P("rep"),
        ),
        out_specs=P(None, "seq", None, None, None, "rep"),
        check_vma=False,
    )
```

```python
import math

import jax
import jax.numpy as jnp
from jax import lax
from jax.experimental import pallas as pl
from jax.experimental.pallas import tpu as pltpu
from jax.sharding import PartitionSpec as P

GROUPS = 32
FRAMES = 4
TH = 8
TW = 8
TILES = 4
HD = 128
N = 16
Z = 8
TOK = 256
LEN = N * TOK
C = 512
CO = C // N
HALF = CO // 2
TAPS = 27
PLANE = 9 * C
BQ = 512
BK = 512
EXTRA = 16
STEPS = LEN // BQ
PITCH = 24
BF = jnp.bfloat16
F32 = jnp.float32
MESH = pl.DeviceIdType.MESH
CORNERS = 4 * FRAMES * TW
RIMS = (
    (32, 32, 1, 0), (0, 32, -1, 0), (96, 32, 0, 1), (64, 32, 0, -1),
    (CORNERS + 48, 16, 1, 1), (CORNERS + 32, 16, 1, -1), (CORNERS + 16, 16, -1, 1), (CORNERS, 16, -1, -1),
)
RIM_ROWS = CORNERS + 4 * 16
CH = C // 2


def unit_kernel(
    q_ref, k_ref, v_ref, taps_ref, wp_ref, gain_ref, shift_ref, bias_ref, out_ref,
    q_raw, k_raw, v_raw, by_token, q_out, k_out, v_out,
    q_all, k_all, v_all, v_t, s_even, s_odd, m_buf, q_t, acc, o_buf, att, wp,
    w_all, lat, by_lanes, edges, rims, stat, stats, moments, field, ones, by_frame, out_t, gathered,
    q_send, q_recv, k_send, k_recv, v_send, v_recv, o_send, o_recv,
    raw_in, w_own, w_send, w_recv, c_send, c_recv, e_send, e_recv, t_send, t_recv, b_send, b_recv, y_send, y_recv,
):
    me = lax.axis_index("seq")
    rep = lax.axis_index("rep")
    x_hi = rep // Z
    z = lax.rem(rep, Z)
    half = lax.rem(me, 2)
    other_core = me + 1 - 2 * half
    twin = me + 2 - 4 * lax.rem(me // 2, 2)
    beside = {"seq": twin, "rep": lax.rem(rep + Z, N)}

    def along_z(d):
        return x_hi * Z + lax.rem(z + d + Z, Z)

    barrier = pltpu.get_barrier_semaphore()

    def greet(t, carry):
        pl.semaphore_signal(
            barrier, inc=1, device_id={"seq": lax.rem(me + t, N)}, device_id_type=MESH
        )
        return carry

    def greet_z(t, carry):
        for seq in (me, twin):
            pl.semaphore_signal(
                barrier, inc=1, device_id={"seq": seq, "rep": along_z(t)}, device_id_type=MESH
            )
        return carry

    lax.fori_loop(1, N, greet, 0)
    lax.fori_loop(1, Z, greet_z, 0)
    pl.semaphore_signal(barrier, inc=1, device_id=beside, device_id_type=MESH)

    k_in = pltpu.make_async_copy(k_ref, k_raw, raw_in.at[0])
    v_in = pltpu.make_async_copy(v_ref, v_raw, raw_in.at[1])
    q_in = pltpu.make_async_copy(q_ref, q_raw, raw_in.at[2])
    wp_in = pltpu.make_async_copy(wp_ref, wp, raw_in.at[3])
    k_in.start()
    v_in.start()
    q_in.start()
    wp_in.start()

    def ds(start, size):
        return pl.ds(pl.multiple_of(start, size), size)

    def own_tap(t):
        return pltpu.make_async_copy(
            taps_ref.at[t],
            w_all.at[t // 9, ds(z * CO, CO), ds(lax.rem(t, 9) * C, C)],
            w_own.at[t],
        )

    def tap_start(t, carry):
        own_tap(t).start()
        return carry

    lax.fori_loop(0, TAPS, tap_start, 0)
    square = (CO, CO)
    on = lax.broadcasted_iota(jnp.int32, square, 0) == lax.broadcasted_iota(jnp.int32, square, 1)
    bias = jnp.sum(
        jnp.where(on, jnp.broadcast_to(bias_ref[...], square), 0.0), axis=1, keepdims=True
    )
    high = bias.astype(BF).astype(F32)
    middle = (bias - high).astype(BF).astype(F32)
    low = bias - high - middle
    lane = lax.broadcasted_iota(jnp.int32, (CO, HD), 1)
    nought = jnp.zeros((CO, HD), F32)
    parts = jnp.where(lane == 0, high, jnp.where(lane == 1, middle, jnp.where(lane == 2, low, nought)))
    w_all[0, ds(z * CO, CO), PLANE:] = nought.astype(BF)
    w_all[1, ds(z * CO, CO), PLANE:] = nought.astype(BF)
    w_all[2, ds(z * CO, CO), PLANE:] = parts.astype(BF)
    v_t[HD:] = jnp.ones((EXTRA, LEN), BF)

    def by_head(copy, raw, out):
        copy.wait()

        def widen(b, carry):
            by_token[ds(b * TOK, TOK)] = raw[ds(b * TOK, TOK)].astype(F32)
            return carry

        lax.fori_loop(0, N, widen, 0)
        for h in range(N):
            out[h] = by_token[pl.ds(h, TOK, stride=N)].astype(BF)

    by_head(k_in, k_raw, k_out)
    pl.semaphore_wait(barrier, N + 2 * (Z - 1))

    def k_copy(t):
        to = lax.rem(me + t, N)
        return pltpu.make_async_remote_copy(
            src_ref=k_out.at[to], dst_ref=k_all.at[ds(me * TOK, TOK)],
            send_sem=k_send.at[t], recv_sem=k_recv.at[t],
            device_id={"seq": to}, device_id_type=MESH,
        )

    def v_copy(t):
        to = lax.rem(me + t, N)
        return pltpu.make_async_remote_copy(
            src_ref=v_out.at[to], dst_ref=v_all.at[ds(me * TOK, TOK)],
            send_sem=v_send.at[t], recv_sem=v_recv.at[t],
            device_id={"seq": to}, device_id_type=MESH,
        )

    def q_copy(t):
        to = lax.rem(me - t + N, N)
        return pltpu.make_async_remote_copy(
            src_ref=q_out.at[to], dst_ref=q_all.at[ds(t * TOK, TOK)],
            send_sem=q_send.at[t], recv_sem=q_recv.at[t],
            device_id={"seq": to}, device_id_type=MESH,
        )

    def o_copy(t):
        to = lax.rem(me + t, N)
        return pltpu.make_async_remote_copy(
            src_ref=o_buf.at[ds(t * TOK, TOK)], dst_ref=att.at[:, ds(me * HD, HD)],
            send_sem=o_send.at[t], recv_sem=o_recv.at[t],
            device_id={"seq": to}, device_id_type=MESH,
        )

    def every(act, copy, first=1, last=N):
        def body(t, carry):
            getattr(copy(t), act)()
            return carry
        lax.fori_loop(first, last, body, 0)

    pieces = [(-d, 1) for d in (1, 2, 3, 4)] + [(d, -1) for d in (1, 2, 3)]

    def shard_rows(d):
        return ds(lax.rem(z + d + Z, Z) * CO + half * HALF, HALF)

    def w_copy(i):
        d, turn = pieces[i]
        held = shard_rows(d + turn)
        return pltpu.make_async_remote_copy(
            src_ref=w_all.at[:, held], dst_ref=w_all.at[:, held],
            send_sem=w_send.at[i], recv_sem=w_recv.at[i],
            device_id={"rep": along_z(turn)}, device_id_type=MESH,
        )

    def core_copy(i):
        held = shard_rows(pieces[i][0])
        return pltpu.make_async_remote_copy(
            src_ref=w_all.at[:, held], dst_ref=w_all.at[:, held],
            send_sem=c_send.at[i], recv_sem=c_recv.at[i],
            device_id={"seq": other_core}, device_id_type=MESH,
        )

    def relay(i, *onward):
        w_copy(i).wait_recv()
        for j in onward:
            w_copy(j).start()
        core_copy(i).start()

    every("start", k_copy)
    every("wait", own_tap, 0, TAPS)
    w_copy(0).start()
    w_copy(4).start()
    by_head(v_in, v_raw, v_out)
    every("start", v_copy)
    by_head(q_in, q_raw, q_out)
    every("start", q_copy)

    def flip(place, block):
        v_t[:HD, place] = jnp.transpose(block)

    mine = ds(me * TOK, TOK)
    k_all[mine] = k_out[me]
    flip(mine, v_out[me])
    q_all[:TOK] = q_out[me]
    every("wait_recv", k_copy)

    factor = HD ** (-0.5) * math.log2(math.e)

    def query_block(u):
        q_t[...] = jnp.transpose(q_all[ds(u * BQ, BQ)])

    def scores(s_buf, keys, top):
        s = jnp.dot(k_all[keys], q_t[...], preferred_element_type=F32)
        s_buf[keys] = s
        return jnp.maximum(top, jnp.max(s.reshape(BK // 8, 8, BQ), axis=0))

    lowest = jnp.full((8, BQ), -jnp.inf, F32)

    def settle(top):
        m_buf[...] = jnp.broadcast_to(jnp.max(top, axis=0, keepdims=True), (8, BQ))

    def exps(s_buf, keys, m):
        below = s_buf[keys].reshape(BK // 8, 8, BQ) - m[None]
        return jnp.exp2(below * factor).reshape(BK, BQ).astype(BF)

    def weigh(p, keys):
        acc[...] += jnp.dot(v_t[:, keys], p, preferred_element_type=F32)

    def emit(u):
        o = (acc[:HD] / acc[HD : HD + 1]).astype(BF)
        o_buf[ds(u * BQ, BQ)] = jnp.transpose(o)

    def step(u, now, then):
        if then is not None:
            q_copy(2 * u + 2).wait_recv()
            q_copy(2 * u + 3).wait_recv()
            query_block(u + 1)
        m = m_buf[...]
        acc[...] = jnp.zeros_like(acc)

        def chunk(c, top):
            keys = ds(c * BK, BK)
            p = exps(now, keys, m)
            if then is not None:
                top = scores(then, keys, top)
            weigh(p, keys)
            return top

        top = lax.fori_loop(0, LEN // BK, chunk, lowest, unroll=2)
        if then is not None:
            settle(top)
        emit(u)

    q_copy(1).wait_recv()
    query_block(0)
    settle(
        lax.fori_loop(
            0, LEN // BK, lambda c, top: scores(s_even, ds(c * BK, BK), top), lowest
        )
    )
    relay(0, 1)
    relay(4, 5)

    def v_arrive(t, carry):
        v_copy(t).wait_recv()
        place = ds(lax.rem(me - t + N, N) * TOK, TOK)
        flip(place, v_all[place])
        return carry

    lax.fori_loop(1, N, v_arrive, 0)
    relay(1, 2)
    relay(5, 6)

    def steps(i, carry):
        step(2 * i, s_even, s_odd)

        @pl.when(i > 0)
        def _():
            o_copy(4 * i).start()

        o_copy(4 * i + 1).start()

        step(2 * i + 1, s_odd, s_even)
        o_copy(4 * i + 2).start()
        o_copy(4 * i + 3).start()

        @pl.when(i == 0)
        def _():
            relay(2, 3)
            relay(6)

        @pl.when(i == 2)
        def _():
            relay(3)

        return carry

    lax.fori_loop(0, STEPS // 2 - 1, steps, 0)
    step(STEPS - 2, s_even, s_odd)
    o_copy(N - 4).start()
    o_copy(N - 3).start()
    step(STEPS - 1, s_odd, None)
    o_copy(N - 2).start()
    o_copy(N - 1).start()
    own_o = pltpu.make_async_copy(o_buf.at[pl.ds(0, TOK)], att.at[:, ds(me * HD, HD)], o_recv.at[0])
    own_o.start()
    own_o.wait()
    every("wait_recv", o_copy)

    wp_in.wait()
    latent = jnp.dot(att[...], wp[...], preferred_element_type=F32).astype(BF)
    wide = latent.astype(F32)
    line = lax.broadcasted_iota(jnp.int32, (8, C), 0)
    stat[...] = jnp.where(
        line == 0,
        jnp.sum(wide, axis=0, keepdims=True),
        jnp.where(line == 1, jnp.sum(wide * wide, axis=0, keepdims=True), 0.0),
    )

    def stat_copy(t):
        return pltpu.make_async_remote_copy(
            src_ref=stat, dst_ref=stats.at[me],
            send_sem=t_send.at[t], recv_sem=t_recv.at[t],
            device_id={"seq": lax.rem(me + t, N)}, device_id_type=MESH,
        )

    every("start", stat_copy)
    lat[0] = latent
    lat_copy = pltpu.make_async_remote_copy(
        src_ref=lat.at[0], dst_ref=lat.at[1], send_sem=b_send.at[0], recv_sem=b_recv.at[0],
        device_id=beside, device_id_type=MESH,
    )
    lat_copy.start()
    for f in range(FRAMES):
        first, last = f * TH * TW, (f + 1) * TH * TW - TW
        edges[pl.ds(f * TW, TW)] = wide[first : first + TW].astype(BF)
        edges[pl.ds((FRAMES + f) * TW, TW)] = wide[last : last + TW].astype(BF)
    for j in range(C // HD):
        lanes = pl.ds(j * HD, HD)
        by_lanes[j] = wide[:, j * HD : (j + 1) * HD]
        edges[pl.ds(64, 32), lanes] = by_lanes[j, pl.ds(0, FRAMES * TH, stride=TW)].astype(BF)
        edges[pl.ds(96, 32), lanes] = by_lanes[j, pl.ds(TW - 1, FRAMES * TH, stride=TW)].astype(BF)
        for n, start in enumerate((0, TW - 1, TW, 2 * TW - 1)):
            corner = by_lanes[j, pl.ds(start, 16, stride=2 * TW)]
            edges[pl.ds(CORNERS + 16 * n, 16), lanes] = corner.astype(BF)

    row, column = me // TILES, lax.rem(me, TILES)

    def rim_rows(n):
        return pl.ds(n * 32, 32) if n < 4 else pl.ds(CORNERS + (n - 4) * 16, 16)

    def rim_copy(n):
        at, size, down, right = RIMS[n]
        to = lax.rem(row + down + TILES, TILES) * TILES + lax.rem(column + right + TILES, TILES)
        return pltpu.make_async_remote_copy(
            src_ref=edges.at[pl.ds(at, size)], dst_ref=rims.at[0, rim_rows(n)],
            send_sem=e_send.at[n], recv_sem=e_recv.at[n],
            device_id={"seq": to}, device_id_type=MESH,
        )

    for n in range(len(RIMS)):
        rim_copy(n).start()
    stats[me] = stat[...]
    ones[...] = jnp.where(
        lax.broadcasted_iota(jnp.int32, (128, TOK), 0) < 3, 1.0, 0.0
    ).astype(BF)
    gain, shift = gain_ref[...], shift_ref[...]
    every("wait_recv", stat_copy)

    size = C // GROUPS
    total = jnp.sum(stats[...], axis=0)
    lane = lax.broadcasted_iota(jnp.int32, (8, C), 1)
    for hop in (1, 2, 4, 8):
        after = pltpu.roll(total, C - hop, 1)
        before = pltpu.roll(total, hop, 1)
        total = total + jnp.where(lax.rem(lane // hop, 2) == 0, after, before)
    total = total / (LEN * size)
    mean = total[0:1]
    var = total[1:2] - mean * mean
    moments[0] = jnp.where(line == 0, mean, jnp.where(line == 1, lax.rsqrt(var + 1e-06), 0.0))

    def to_beside(n, ref):
        return pltpu.make_async_remote_copy(
            src_ref=ref.at[0], dst_ref=ref.at[1], send_sem=b_send.at[n], recv_sem=b_recv.at[n],
            device_id=beside, device_id_type=MESH,
        )

    moments_copy = to_beside(1, moments)
    rims_copy = to_beside(2, rims)
    moments_copy.start()
    for n in range(len(RIMS)):
        rim_copy(n).wait_recv()
    rims_copy.start()

    def decode(which, tile):
        mean, inverse = moments[which, 0:1], moments[which, 1:2]

        def activate(x):
            return jax.nn.silu((x.astype(F32) - mean) * inverse * gain + shift)

        inner = activate(lat[which])
        for f in range(FRAMES):
            for h in range(TH):
                field[f * (TH + 2) + 1 + h, pl.ds(8, TW)] = inner[
                    (f * TH + h) * TW : (f * TH + h + 1) * TW
                ]

        row, column = tile // TILES, lax.rem(tile, TILES)
        above, below = row > 0, row < TILES - 1
        before, after = column > 0, column < TILES - 1
        inside = (
            above, below, before, after,
            above & before, above & after, below & before, below & after,
        )
        for n in range(len(RIMS)):
            rim = jnp.where(inside[n], activate(rims[which, rim_rows(n)]), 0.0)
            for f in range(FRAMES):
                first = f * (TH + 2)
                last = first + TH + 1
                if n < 2:
                    field[last if n else first, pl.ds(8, TW)] = rim[f * TW : (f + 1) * TW]
                elif n < 4:
                    for h in range(TH):
                        k = f * TH + h
                        field[first + h + 1, pl.ds(7 if n == 2 else 16, 1)] = rim[k : k + 1]
                else:
                    k = 4 * f + (3 if n < 6 else 0)
                    side = 7 if n in (4, 6) else 16
                    field[first if n < 6 else last, pl.ds(side, 1)] = rim[k : k + 1]

        if which == 0:
            for i in range(len(pieces)):
                core_copy(i).wait_recv()
        by_frame[:2] = jnp.zeros((2, CH, TOK), F32)
        by_frame[2] = jnp.transpose(lat[which, :, ds(x_hi * CH, CH)]).astype(F32) + jnp.dot(
            w_all[2, :, PLANE:], ones[...], preferred_element_type=F32
        )

        def convolve(r, carry):
            x = jnp.concatenate(
                [
                    jnp.transpose(
                        jnp.concatenate(
                            [
                                field[r + (f * (TH + 2) + h), pl.ds(7 + s, TW)]
                                for f in range(FRAMES)
                                for h in range(TH)
                            ],
                            axis=0,
                        ).astype(BF)
                    )
                    for s in range(3)
                ],
                axis=0,
            )
            w = w_all[:, :, ds(r * 3 * C, 3 * C)].reshape(3 * CH, 3 * C)
            part = jnp.dot(w, x, preferred_element_type=F32)
            by_frame[...] += part.reshape(3, CH, TOK)
            return carry

        lax.fori_loop(0, 3, convolve, 0)
        at = lax.broadcasted_iota(jnp.int32, (CH, TOK), 1)
        frame = TH * TW
        one = jnp.where(at >= frame, pltpu.roll(by_frame[1], frame, 1), 0.0)
        two = jnp.where(at >= 2 * frame, pltpu.roll(by_frame[0], 2 * frame, 1), 0.0)
        out_t[which] = (by_frame[2] + one + two).astype(BF)

    def y_copy(t):
        theirs, hop = t // Z, lax.rem(t, Z)
        video = lax.rem(rep + theirs * Z, N)
        return pltpu.make_async_remote_copy(
            src_ref=out_t.at[theirs, ds(lax.rem(z + hop, Z) * CO, CO)], dst_ref=gathered.at[video],
            send_sem=y_send.at[t], recv_sem=y_recv.at[t],
            device_id={"seq": me + theirs * (twin - me), "rep": along_z(hop)},
            device_id_type=MESH,
        )

    decode(0, me)
    every("start", y_copy, 1, Z)
    gathered[rep] = out_t[0, ds(z * CO, CO)]
    lat_copy.wait_recv()
    moments_copy.wait_recv()
    rims_copy.wait_recv()
    decode(1, twin)
    every("start", y_copy, Z, N)
    for i in range(len(pieces)):
        w_copy(i).wait_send()
        core_copy(i).wait_send()
    for n in range(len(RIMS)):
        rim_copy(n).wait_send()
    lat_copy.wait_send()
    moments_copy.wait_send()
    rims_copy.wait_send()
    every("wait_send", k_copy)
    every("wait_send", v_copy)
    every("wait_send", q_copy)
    every("wait_send", o_copy)
    every("wait_send", stat_copy)
    every("wait_recv", y_copy)
    out_ref[...] = gathered[...]
    every("wait_send", y_copy)


def unit(q, k, v, taps, w_proj, gain, shift, bias):
    sem = pltpu.SemaphoreType.DMA
    vmem = pl.BlockSpec(memory_space=pltpu.VMEM)
    return pl.pallas_call(
        unit_kernel,
        out_shape=jax.ShapeDtypeStruct((N, CO, TOK), BF),
        in_specs=[pl.BlockSpec(memory_space=pl.ANY)] * 5 + [vmem] * 3,
        out_specs=vmem,
        scratch_shapes=[
            pltpu.VMEM((LEN, HD), BF),
            pltpu.VMEM((LEN, HD), BF),
            pltpu.VMEM((LEN, HD), BF),
            pltpu.VMEM((LEN, HD), F32),
            pltpu.VMEM((N, TOK, HD), BF),
            pltpu.VMEM((N, TOK, HD), BF),
            pltpu.VMEM((N, TOK, HD), BF),
            pltpu.VMEM((LEN, HD), BF),
            pltpu.VMEM((LEN, HD), BF),
            pltpu.VMEM((LEN, HD), BF),
            pltpu.VMEM((HD + EXTRA, LEN), BF),
            pltpu.VMEM((LEN, BQ), F32),
            pltpu.VMEM((LEN, BQ), F32),
            pltpu.VMEM((8, BQ), F32),
            pltpu.VMEM((HD, BQ), BF),
            pltpu.VMEM((HD + EXTRA, BQ), F32),
            pltpu.VMEM((LEN, HD), BF),
            pltpu.VMEM((TOK, N * HD), BF),
            pltpu.VMEM((N * HD, C), BF),
            pltpu.VMEM((3, CH, PLANE + 128), BF),
            pltpu.VMEM((2, TOK, C), BF),
            pltpu.VMEM((C // HD, TOK, HD), F32),
            pltpu.VMEM((RIM_ROWS, C), BF),
            pltpu.VMEM((2, RIM_ROWS, C), BF),
            pltpu.VMEM((8, C), F32),
            pltpu.VMEM((N, 8, C), F32),
            pltpu.VMEM((2, 8, C), F32),
            pltpu.VMEM((FRAMES * (TH + 2), PITCH, C), F32),
            pltpu.VMEM((128, TOK), BF),
            pltpu.VMEM((3, CH, TOK), F32),
            pltpu.VMEM((2, CH, TOK), BF),
            pltpu.VMEM((N, CO, TOK), BF),
        ]
        + [sem((N,))] * 8
        + [sem((4,)), sem((TAPS,))]
        + [sem((7,))] * 4
        + [sem((len(RIMS),))] * 2
        + [sem((N,))] * 2
        + [sem((3,))] * 2
        + [sem((N,))] * 2,
        compiler_params=pltpu.CompilerParams(
            collective_id=0, has_side_effects=True, vmem_limit_bytes=62 * 2**20
        ),
        cost_estimate=pl.CostEstimate(
            flops=4 * LEN * LEN * HD + 2 * TOK * TAPS * C * C,
            bytes_accessed=8 * 2**20,
            transcendentals=LEN * LEN,
        ),
        name="unit",
    )(q, k, v, taps, w_proj, gain, shift, bias)


def shards(queries, keys, values, w_proj, norm_gain, norm_bias, conv_weight, conv_bias):
    taps = conv_weight.reshape(TAPS, C, CO).transpose(0, 2, 1)
    q, k, v = (a.reshape(LEN, HD) for a in (queries, keys, values))
    out = unit(
        q, k, v, taps, w_proj, norm_gain[None], norm_bias[None], conv_bias[None]
    )
    return out.transpose(0, 2, 1).reshape(N, 1, FRAMES, TH, TW, CO)


def solution(mesh):
    return jax.shard_map(
        shards,
        mesh=mesh,
        in_specs=(
            P("rep", "seq", None, None),
            P("rep", "seq", None, None),
            P("rep", "seq", None, None),
            P(),
            P(),
            P(),
            P(None, None, None, None, "rep"),
            P("rep"),
        ),
        out_specs=P(None, "seq", None, None, None, "rep"),
        check_vma=False,
    )
```
